128 devices in a mesh: grp: 8 (over x, core), tile: 16 (over y, z).
Axes of the slice: x: 4, y: 4, z: 4, core: 2. Of those that a mesh axis runs over, the one named last changes fastest.
Arguments:
- molecule_coords: float32 [3, 2097152], P(None, ('grp', 'tile')), may hold values from 0 to 1.6
- molecule_speeds: float32 [3, 2097152], P(None, ('grp', 'tile')), may hold values from -6 to 6
- molecule_thermal_state: float32 [2097152], P(('grp', 'tile')), may hold values from 0.5 to 2
- conservative_strength: float32 [2097152], P(('grp', 'tile')), may hold values from 0.05 to 0.5
- noise_keys: int32 [2097152], P(('grp', 'tile')), may hold values from 0 to 32767
- exported_tile_places: int32 [128, 16, 12], P(('grp', 'tile')), may hold values from 0 to 127
- tile_couplings: int32 [128, 1024, 2], P(('grp', 'tile')), may hold values from 0 to 383, as said below
- processor_coupling_tally: int32 [128], P(('grp', 'tile')), may hold values from 512 to 1024
Outputs:
- force_heat: float32 [4, 2097152], P(None, ('grp', 'tile'))
The draws below stay inside these ranges and needn't reach their ends.
Inputs may be any that keep to these rules, and one draw needn't show every extreme that they name: `tile_couplings`: second slots of workers in the lowest slab are below 192; first slots are below 192.
All inputs are finite; a program needn't handle non-finite values.
Results may differ from the reference program's by a relative error of at most 0.0003.
Values sent between devices are 32-bit elements; how exact they have to be, the bound alone decides.
A program may use at most 128 MiB of HBM per device.

```python
import math
import jax
import jax.numpy as jnp
from jax import lax

BLK_DEV = 128
CAP = 12
PAIR_CAP = 1024
GRAND_MOLECULES = 2097152
N_GRP = 8
N_TILE = 16


def draw_tile_couplings(key, part):
    worker_units = N_GRP * N_TILE
    buffer_len = N_TILE * CAP
    first = jax.random.randint(jax.random.fold_in(key, 1), (worker_units, PAIR_CAP), 0, buffer_len)
    second = jax.random.randint(jax.random.fold_in(key, 2), (worker_units, PAIR_CAP), 0, 2 * buffer_len)
    groups = jnp.arange(worker_units) // N_TILE
    second = jnp.where(groups[:, None] == 0, second % buffer_len, second)
    chosen = jax.random.randint(jax.random.fold_in(key, 3), (), N_TILE, worker_units)
    lowest = jax.random.randint(jax.random.fold_in(key, 4), (), 0, worker_units)
    first = first.at[chosen, 0].set(buffer_len - 1).at[lowest, 0].set(0)
    second = second.at[chosen, 0].set(2 * buffer_len - 1).at[lowest, 1].set(0)
    return jnp.stack([first, second], 2).astype(jnp.int32)


def draw_processor_coupling_tally(key, part):
    worker_units = N_GRP * N_TILE
    counts = jax.random.randint(jax.random.fold_in(key, 11), (worker_units,), PAIR_CAP // 2, PAIR_CAP + 1)
    dense = jax.random.randint(jax.random.fold_in(key, 12), (worker_units,), 0, 4) == 0
    counts = jnp.where(dense, PAIR_CAP, counts)
    chosen = jax.random.randint(jax.random.fold_in(key, 13), (), 0, worker_units)
    lowest = jax.random.randint(jax.random.fold_in(key, 14), (), 0, worker_units)
    counts = counts.at[lowest].set(PAIR_CAP // 2)
    return counts.at[chosen].set(PAIR_CAP).astype(jnp.int32)


def with_ends(entries, rng, smallest, high):
    place = [jax.random.randint(jax.random.fold_in(rng, axis), (), 0, length) for axis, length in enumerate(entries.shape)]
    main_axis = entries.shape.index(max(entries.shape))
    beside = place[:main_axis] + [(place[main_axis] + 1) % entries.shape[main_axis]] + place[main_axis + 1:]
    return entries.at[tuple(place)].set(smallest).at[tuple(beside)].set(high)


def shard_levels(rng, extent, shards, least, largest):
    level, own = 1.0, jax.random.fold_in(rng, 6)
    for axis_at, shards_of in shards:
        draws = jnp.exp(jax.random.uniform(jax.random.fold_in(own, axis_at), (shards_of,), jnp.float32, least / len(shards), largest / len(shards)))
        level = level * jnp.repeat(draws, extent[axis_at] // shards_of).reshape([-1 if axis == axis_at else 1 for axis in range(len(extent))])
    return level


def gaussian(own_key, extent, width, limit, split=(), kind=jnp.bfloat16):
    gain = shard_levels(own_key, extent, split, -0.22, 0.18) if split else 1.0
    drawn = jax.random.normal(own_key, extent, jnp.float32) * width * gain
    return jnp.minimum(jnp.maximum(drawn, -limit), limit).astype(kind)


def setup_inputs(seed: int = 0) -> dict:
    arg_keys = jax.random.split(jax.random.key(seed), 9)
    return {
        "molecule_coords": jnp.clip(1.6 * jax.random.uniform(arg_keys[0], (3, GRAND_MOLECULES), jnp.float32) ** shard_levels(arg_keys[0], (3, GRAND_MOLECULES), ((1, 128),), -0.2, 0.2), 0.0, 1.6),
        "molecule_speeds": gaussian(arg_keys[1], (3, GRAND_MOLECULES), 1.0, 6.0, ((1, 128),), jnp.float32),
        "molecule_thermal_state": jnp.clip(0.5 + 1.5 * jax.random.uniform(arg_keys[2], (GRAND_MOLECULES,), jnp.float32) ** shard_levels(arg_keys[2], (GRAND_MOLECULES,), ((0, 128),), -0.2, 0.2), 0.5, 2.0),
        "conservative_strength": jnp.clip(jnp.exp(math.log(0.5) - 2.3025851 * jax.random.uniform(arg_keys[3], (GRAND_MOLECULES,), jnp.float32) ** shard_levels(arg_keys[3], (GRAND_MOLECULES,), ((0, 128),), -0.2, 0.2)), 0.05, 0.5),
        "noise_keys": with_ends(jax.random.randint(arg_keys[4], (GRAND_MOLECULES,), 0, 32768), jax.random.fold_in(arg_keys[4], 1), 0, 32767).astype(jnp.int32),
        "exported_tile_places": with_ends(jax.random.randint(arg_keys[5], (N_GRP * N_TILE, N_TILE, CAP), 0, BLK_DEV), jax.random.fold_in(arg_keys[5], 1), 0, BLK_DEV - 1).astype(jnp.int32),
        "tile_couplings": draw_tile_couplings(jax.random.fold_in(arg_keys[8], 71), 0),
        "processor_coupling_tally": draw_processor_coupling_tally(jax.random.fold_in(arg_keys[8], 71), 0),
    }


friction = 0.45
noise_amp = 0.3
conductivity = 0.1

def tile_pair(first, second):
    offset = first[0:3, :, None] - second[0:3, None, :]
    radius = jnp.sqrt(lax.optimization_barrier(jnp.sum(offset * offset, 0)) + 0.01)
    unit = offset / radius
    weight = jnp.maximum(1.0 - radius, 0.0)
    relative = first[3:6, :, None] - second[3:6, None, :]
    along = lax.optimization_barrier(jnp.sum(unit * relative, 0))
    repulse = 0.5 * (first[7][:, None] + second[7][None, :])
    seed_first = first[8].astype(jnp.int32)
    seed_second = second[8].astype(jnp.int32)
    hashed = (seed_first[:, None] * seed_second[None, :] + seed_first[:, None] + seed_second[None, :]) % 65521
    noise = hashed.astype(jnp.float32) * (2.0 / 65521.0) - 1.0
    magnitude = repulse * weight - friction * weight * weight * along + noise_amp * weight * noise
    force = magnitude[None] * unit
    conduct = conductivity * weight * weight * (second[6][None, :] - first[6][:, None])
    viscous = 0.5 * friction * weight * weight * along * along
    on_first = jnp.concatenate([lax.optimization_barrier(jnp.sum(force, 2)), lax.optimization_barrier(jnp.sum(conduct + viscous, 1))[None]], 0)
    on_second = jnp.concatenate([-lax.optimization_barrier(jnp.sum(force, 1)), lax.optimization_barrier(jnp.sum(viscous - conduct, 0))[None]], 0)
    return (on_first, on_second)

def tile_self(block_data):
    offset = block_data[0:3, :, None] - block_data[0:3, None, :]
    radius = jnp.sqrt(lax.optimization_barrier(jnp.sum(offset * offset, 0)) + 0.01)
    unit = offset / radius
    weight = jnp.maximum(1.0 - radius, 0.0)
    relative = block_data[3:6, :, None] - block_data[3:6, None, :]
    along = lax.optimization_barrier(jnp.sum(unit * relative, 0))
    repulse = 0.5 * (block_data[7][:, None] + block_data[7][None, :])
    seed_first = block_data[8].astype(jnp.int32)
    hashed = (seed_first[:, None] * seed_first[None, :] + seed_first[:, None] + seed_first[None, :]) % 65521
    noise = hashed.astype(jnp.float32) * (2.0 / 65521.0) - 1.0
    others = 1.0 - jnp.eye(block_data.shape[1], dtype=jnp.float32)
    magnitude = (repulse * weight - friction * weight * weight * along + noise_amp * weight * noise) * others
    force = magnitude[None] * unit
    conduct = conductivity * weight * weight * (block_data[6][None, :] - block_data[6][:, None])
    viscous = 0.5 * friction * weight * weight * along * along
    heating = lax.optimization_barrier(jnp.sum((conduct + viscous) * others, 1))
    return jnp.concatenate([lax.optimization_barrier(jnp.sum(force, 2)), heating[None]], 0)

def reference(molecule_coords, molecule_speeds, molecule_thermal_state, conservative_strength, noise_keys, exported_tile_places, tile_couplings, processor_coupling_tally):
    nblocks = molecule_coords.shape[1] // 128
    molecule_entries = jnp.concatenate([molecule_coords, molecule_speeds, molecule_thermal_state[None], conservative_strength[None], noise_keys[None].astype(jnp.float32)], 0)
    molecule_entries = molecule_entries.reshape(9, nblocks, 128).transpose(1, 0, 2)
    worker_units = N_GRP * N_TILE
    workers = jnp.arange(worker_units, dtype=jnp.int32)
    groups = workers // N_TILE
    owners = groups[:, None, None] * N_TILE + jnp.arange(N_TILE, dtype=jnp.int32)[None, :, None]
    column_list = jnp.arange(CAP, dtype=jnp.int32)[None, None, :]
    slot_blocks = exported_tile_places[owners, (workers % N_TILE)[:, None, None], column_list]
    held_ids = (owners * BLK_DEV + slot_blocks).reshape(worker_units, N_TILE * CAP)
    lower = jnp.maximum(workers - N_TILE, 0)
    buffer_len = N_TILE * CAP
    first_ids = jnp.take_along_axis(held_ids, tile_couplings[:, :, 0], 1)
    second_slot = tile_couplings[:, :, 1]
    near_ids = jnp.take_along_axis(held_ids, jnp.minimum(second_slot, buffer_len - 1), 1)
    far_ids = jnp.take_along_axis(held_ids[lower], jnp.maximum(second_slot - buffer_len, 0), 1)
    second_ids = jnp.where(second_slot < buffer_len, near_ids, far_ids)
    active = (jnp.arange(PAIR_CAP, dtype=jnp.int32)[None, :] < processor_coupling_tally[:, None]).astype(jnp.float32)
    batch = 256
    first_ids = first_ids.reshape(-1, batch)
    second_ids = second_ids.reshape(-1, batch)
    active = active.reshape(-1, batch)

    def consume(accum, items):
        first_blk, second_blk, live = items
        on_first, on_second = jax.vmap(tile_pair)(molecule_entries[first_blk], molecule_entries[second_blk])
        live = live[:, None, None]
        accum = accum.at[first_blk].add(on_first * live)
        accum = accum.at[second_blk].add(on_second * live)
        return (accum, None)
    accum = jnp.zeros((nblocks, 4, 128), jnp.float32)
    accum, _ = lax.scan(consume, accum, (first_ids, second_ids, active))

    def self_step(carry, group_data):
        return (carry, jax.vmap(tile_self)(group_data))
    _, selfs = lax.scan(self_step, jnp.zeros((), jnp.float32), molecule_entries.reshape(-1, BLK_DEV, 9, 128))
    accum = accum + selfs.reshape(nblocks, 4, 128)
    return accum.transpose(1, 0, 2).reshape(4, nblocks * 128)
```

```python
import functools

import jax
import jax.numpy as jnp
from jax import lax
from jax.experimental import pallas as pl
from jax.experimental.pallas import tpu as pltpu
from jax.sharding import PartitionSpec as P

friction = 0.45
noise_amp = 0.3
conductivity = 0.1
MODULUS = 65521
MIDDLE = 0.8

F32 = jnp.float32
BF16 = jnp.bfloat16
I32 = jnp.int32
MESH = pl.DeviceIdType.MESH
MIB = 2**20

HASH_UNIT = 2.0**32
FORCE_UNIT = 2.0 * noise_amp / HASH_UNIT
PULL = friction / FORCE_UNIT
HEAT_UNIT = 0.5 * friction / (PULL * PULL)
WARM = conductivity / HEAT_UNIT
STRENGTH = 0.5 / FORCE_UNIT
STRENGTH_SHIFT = -0.5 / MODULUS * HASH_UNIT

GROUP_ROWS = 8
K_WIDE = 64
K_SLIM = 32


def round_up(value, multiple):
    return (value + multiple - 1) // multiple * multiple


def parts_of(value):
    high = value.astype(BF16).astype(F32)
    rest = value - high
    middle = rest.astype(BF16).astype(F32)
    low = (rest - middle).astype(BF16).astype(F32)
    return high, middle, low


def bead_terms(raw):
    shape = raw.shape
    row = lax.broadcasted_iota(I32, shape, 1)
    position = row < 3
    scale = jnp.where(row < 6, 1.0, jnp.where(row == 6, WARM, STRENGTH)).astype(F32)
    shift = jnp.where(position, -MIDDLE, jnp.where(row == 7, STRENGTH_SHIFT, 0.0)).astype(F32)
    base = raw * scale + shift
    high, middle, low = parts_of(base)
    swapped = jnp.concatenate([base[:, 3:6], base[:, 0:3], jnp.zeros_like(base[:, 0:2])], 1)
    square = jnp.sum(jnp.where(position, base * base, 0.0), 1, keepdims=True) + 0.005
    cross = PULL * jnp.sum(jnp.where(position, base * swapped, 0.0), 1, keepdims=True)
    return row, base, (high, middle, low), swapped, parts_of(square), parts_of(cross)


def rows_of(row, values, first=0):
    out = jnp.zeros(row.shape, F32)
    for at, value in enumerate(values):
        out = jnp.where(row == first + at, value, out)
    return out


def tall_rows(terms):
    row, _, (high, middle, low), _, square, cross = terms
    ones = jnp.ones(row.shape, F32)
    own = rows_of(row, square + cross)
    return jnp.concatenate([high, middle, low, ones, high, high, middle, own], 1)


def wide_rows(terms):
    row, base, (high, middle, low), swapped, square, cross = terms
    near = [jnp.where(row < 3, -2.0 * part, 0.0) for part in (high, middle, low)]
    pull = parts_of(-PULL * swapped)
    one_square = jnp.where(row < 3, 1.0, 0.0).astype(F32)
    one_cross = jnp.where((row >= 3) & (row < 6), 1.0, 0.0).astype(F32)

    def stack(part, theirs, one):
        return jnp.concatenate([part[0]] * 3 + [theirs, part[1], part[2], part[1], one], 1)

    wide = jnp.concatenate(
        [stack(near, rows_of(row, square), one_square), stack(pull, rows_of(row, cross), one_cross)], 2
    )
    one_strength = jnp.where(row == 7, 1.0, 0.0).astype(F32)
    one_warm = jnp.where(row == 6, -1.0, 0.0).astype(F32)
    strengths = rows_of(row, [part[:, 7:8] for part in (high, middle, low)])
    warmths = rows_of(row, [part[:, 6:7] for part in (high, middle, low)])
    slim = jnp.concatenate(
        [
            jnp.concatenate([one_strength] * 3 + [strengths], 1),
            jnp.concatenate([one_warm] * 3 + [warmths], 1),
        ],
        2,
    )
    return wide.astype(BF16), slim.astype(BF16)


def weigh_rows(terms):
    row, _, (high, middle, low), _, _, _ = terms
    second = rows_of(row, [middle[:, at : at + 1] for at in range(3)] + [low[:, at : at + 1] for at in range(3)] + [1.0])
    return jnp.concatenate([high, second], 1).astype(BF16)


def hash_rows(keys):
    whole = int(HASH_UNIT) // MODULUS
    left = int(HASH_UNIT) - whole * MODULUS
    seed = keys + 1.0
    extra = jnp.floor(seed * (left / MODULUS) + 0.5)
    return seed.astype(I32), seed.astype(I32) * whole + extra.astype(I32)


def interactions(tall, wide, slim, seeds, factors):
    first = jnp.dot(tall, wide, preferred_element_type=F32)
    second = jnp.dot(tall[:, :K_SLIM], slim, preferred_element_type=F32)
    radius2, pull = first[:, :128], first[:, 128:]
    strength, warmth = second[:, :128], second[:, 128:]
    turned = seeds * factors + jnp.int32(-(2**31))
    lift = jnp.maximum(lax.rsqrt(radius2) - 1.0, 0.0)
    drag = lift * pull
    gain = lift * (strength + turned.astype(F32) - drag)
    viscous = drag * drag
    conduct = lift * lift * radius2 * warmth
    return gain, viscous + conduct, viscous - conduct


def halves(value):
    high = value.astype(BF16)
    return high, (value - high.astype(F32)).astype(BF16)


def gather_kernel(
    n_grp, n_tile, cap, blocks, places_ref, coords_ref, speeds_ref, temp_ref, strength_ref, keys_ref,
    held_ref, own, box, far_box, send_sems, recv_sems, up_sems, down_sems, near_box,
):
    g, t = lax.axis_index("grp"), lax.axis_index("tile")
    above, below = lax.rem(g + 1, n_grp), lax.rem(g + n_grp - 1, n_grp)
    barrier = pltpu.get_barrier_semaphore()
    for step in range(1, n_tile):
        pl.semaphore_signal(barrier, inc=1, device_id=(g, lax.rem(t + step, n_tile)), device_id_type=MESH)
    pl.semaphore_signal(barrier, inc=1, device_id=(below, t), device_id_type=MESH)

    def pack(b, carry):
        lanes = pl.ds(pl.multiple_of(b * 128, 128), 128)
        own[b, 0:3] = coords_ref[:, lanes]
        own[b, 3:6] = speeds_ref[:, lanes]
        own[b, 6:7] = temp_ref[pl.ds(b, 1)]
        own[b, 7:8] = strength_ref[pl.ds(b, 1)]
        own[b, 8:9] = keys_ref[pl.ds(b, 1)].astype(F32)
        return carry

    lax.fori_loop(0, blocks, pack, 0, unroll=8)

    def fill(worker):
        for c in range(cap):
            place = places_ref[worker * cap + c]
            box[worker, 8 * c : 8 * c + 8] = own[place, 0:8]
            box[worker, 8 * cap + c : 8 * cap + c + 1] = own[place, 8:9]

    def outgoing(step):
        worker = lax.rem(t + step, n_tile)
        return pltpu.make_async_remote_copy(
            src_ref=box.at[worker], dst_ref=near_box.at[t], send_sem=send_sems.at[step], recv_sem=recv_sems.at[t],
            device_id=(g, worker), device_id_type=MESH,
        )

    def incoming(owner):
        return pltpu.make_async_remote_copy(
            src_ref=box.at[owner], dst_ref=near_box.at[owner], send_sem=send_sems.at[0], recv_sem=recv_sems.at[owner],
            device_id=(g, owner), device_id_type=MESH,
        )

    def upward(owner, source):
        return pltpu.make_async_remote_copy(
            src_ref=source.at[owner], dst_ref=far_box.at[owner], send_sem=up_sems.at[owner], recv_sem=down_sems.at[owner],
            device_id=(above, t), device_id_type=MESH,
        )

    pl.semaphore_wait(barrier, n_tile)

    def send(step, carry):
        fill(lax.rem(t + step, n_tile))
        outgoing(step).start()
        return carry

    lax.fori_loop(1, n_tile, send, 0)
    fill(t)
    near_box[t] = box[t]
    upward(t, near_box).start()

    def take(step, carry):
        owner = lax.rem(t + n_tile - step, n_tile)
        incoming(owner).wait_recv()
        upward(owner, near_box).start()
        return carry

    lax.fori_loop(1, n_tile, take, 0)
    held_ref[0:n_tile] = near_box[...]

    def finish(owner, carry):
        copy = upward(owner, near_box)
        copy.wait_send()
        copy.wait_recv()
        return carry

    lax.fori_loop(0, n_tile, finish, 0)

    def sent(step, carry):
        outgoing(step).wait_send()
        return carry

    lax.fori_loop(1, n_tile, sent, 0)
    held_ref[n_tile:] = far_box[...]


def gather_blocks(n_grp, n_tile, cap, blocks, places, coords, speeds, temp, strength, keys):
    rows = round_up(9 * cap, 8)
    box = pltpu.VMEM((n_tile, rows, 128), F32)
    sems = pltpu.SemaphoreType.DMA((n_tile,))
    vmem = pl.BlockSpec(memory_space=pltpu.VMEM)
    return pl.pallas_call(
        functools.partial(gather_kernel, n_grp, n_tile, cap, blocks),
        out_shape=jax.ShapeDtypeStruct((2 * n_tile, rows, 128), F32),
        in_specs=[pl.BlockSpec(memory_space=pltpu.SMEM)] + [vmem] * 5,
        out_specs=vmem,
        scratch_shapes=[pltpu.VMEM((blocks, 16, 128), F32), box, box, sems, sems, sems, sems, box],
        compiler_params=pltpu.CompilerParams(collective_id=0, has_side_effects=True, vmem_limit_bytes=24 * MIB),
        name="gather_blocks",
    )(places, coords, speeds, temp, strength, keys)


def self_kernel(blocks, coords_ref, speeds_ref, temp_ref, strength_ref, keys_ref, out_ref):
    def step(b, carry):
        lanes = pl.ds(pl.multiple_of(b * 128, 128), 128)
        raw = jnp.concatenate(
            [coords_ref[:, lanes], speeds_ref[:, lanes], temp_ref[pl.ds(b, 1)], strength_ref[pl.ds(b, 1)]], 0
        )[None]
        seed, factor = hash_rows(keys_ref[pl.ds(b, 1)].astype(F32))
        terms = bead_terms(raw)
        wide, slim = wide_rows(terms)
        stack = jnp.concatenate([tall_rows(terms)[0], jnp.broadcast_to(seed.astype(F32), (64, 128))], 0).T
        tall = stack[:, :K_WIDE].astype(BF16)
        seeds = jnp.broadcast_to(stack[:, K_WIDE : K_WIDE + 1].astype(I32), (128, 128))
        gain, _, heat = interactions(tall, wide[0], slim[0], seeds, factor)
        high, low = halves(gain)
        weigh = weigh_rows(terms)[0]
        sums = jnp.dot(
            jnp.concatenate([weigh, weigh], 1), jnp.concatenate([high, low], 0), preferred_element_type=F32
        )
        out_ref[b] = result_rows(terms[1][0], sums, jnp.sum(heat, 0, keepdims=True))
        return carry

    lax.fori_loop(0, blocks, step, 0, unroll=2)


def result_rows(base, sums, heat):
    moved = sums[0:3] + sums[8:11] + sums[11:14]
    force = FORCE_UNIT * (base[0:3] * sums[14:15] - moved)
    return jnp.concatenate([force, HEAT_UNIT * heat], 0)


def self_terms(blocks, coords, speeds, temp, strength, keys):
    vmem = pl.BlockSpec(memory_space=pltpu.VMEM)
    return pl.pallas_call(
        functools.partial(self_kernel, blocks),
        out_shape=jax.ShapeDtypeStruct((blocks, 4, 128), F32),
        in_specs=[vmem] * 5,
        out_specs=vmem,
        compiler_params=pltpu.CompilerParams(vmem_limit_bytes=24 * MIB),
        name="self_terms",
    )(coords, speeds, temp, strength, keys)


GANG = 8


def pair_kernel(
    n_tile, cap, pairs_ref, live_ref, held_ref, out_ref,
    tall_s, wide_s, slim_s, weigh_s, seeds_s, factor_s, acc, heat_acc,
):
    slots = n_tile * cap

    def prepare(owner, first, with_tall):
        boxed = held_ref.at[owner]
        raw = boxed[0 : 8 * cap].reshape(cap, 8, 128)
        seed, factor = hash_rows(boxed[8 * cap : 9 * cap])
        for c in range(0, cap, 4):
            slot = first + c
            terms = bead_terms(raw[c : c + 4])
            wide, slim = wide_rows(terms)
            wide_s[pl.ds(slot, 4)] = wide
            slim_s[pl.ds(slot, 4)] = slim
            weigh_s[pl.ds(slot, 4)] = weigh_rows(terms)
            acc[pl.ds(slot, 4)] = jnp.zeros((4, 24, 128), F32)
            for n in range(4):
                factor_s[slot + n] = factor[c + n : c + n + 1]
            if with_tall:
                tall = tall_rows(terms)
                for n in range(4):
                    mine = jnp.broadcast_to(seed[c + n : c + n + 1].astype(F32), (64, 128))
                    stack = jnp.concatenate([tall[n], mine], 0).T
                    tall_s[slot + n] = stack[:, :K_WIDE].astype(BF16)
                    seeds_s[slot + n] = jnp.broadcast_to(stack[:, K_WIDE : K_WIDE + 1].astype(I32), (128, 128))
                    heat_acc[slot + n] = jnp.zeros((128, 128), F32)

    def near_step(owner, carry):
        prepare(owner, owner * cap, True)
        return carry

    def far_step(owner, carry):
        prepare(n_tile + owner, slots + owner * cap, False)
        return carry

    lax.fori_loop(0, n_tile, near_step, 0)
    lax.fori_loop(0, n_tile, far_step, 0)

    live = live_ref[0]

    def gang(step, carry):
        firsts, seconds, results = [], [], []
        for u in range(GANG):
            k = step * GANG + u
            dead = k >= live
            p, q = pairs_ref[2 * k], pairs_ref[2 * k + 1]
            gain, heat_p, heat_q = interactions(tall_s[p], wide_s[q], slim_s[q], seeds_s[p], factor_s[q])
            firsts.append((p, jnp.where(dead, slots, p)))
            seconds.append((q, jnp.where(dead, 2 * slots, q)))
            results.append((halves(gain), heat_p, jnp.sum(heat_q.reshape(16, 8, 128), 0)))
        for u in range(0, GANG, 2):
            (h0, l0), (h1, l1) = results[u][0], results[u + 1][0]
            weigh_p = [weigh_s[firsts[v][0]] for v in (u, u + 1)]
            weigh_q = [weigh_s[seconds[v][0]] for v in (u, u + 1)]
            down = jnp.concatenate([jnp.concatenate([h0, h1], 1), jnp.concatenate([l0, l1], 1)], 0)
            across = jnp.concatenate([jnp.concatenate([h0, l0], 1), jnp.concatenate([h1, l1], 1)], 0)
            left = jnp.concatenate([jnp.concatenate([w, w], 1) for w in weigh_p], 0)
            right = jnp.concatenate([jnp.concatenate([w, w], 1) for w in weigh_q], 0)
            on_q = jnp.dot(left, down, preferred_element_type=F32)
            on_p = lax.dot_general(right, across, (((1,), (1,)), ((), ())), preferred_element_type=F32)
            for v in (0, 1):
                rows, lanes = slice(16 * v, 16 * v + 16), slice(128 * v, 128 * v + 128)
                to_p, to_q = firsts[u + v][1], seconds[u + v][1]
                acc_p = jnp.where(to_p == slots, 2 * slots, to_p)
                acc[acc_p, 0:16] += on_p[rows, lanes]
                acc[to_q, 0:16] += on_q[rows, lanes]
                acc[to_q, 16:24] += results[u + v][2]
                heat_acc[to_p] += results[u + v][1]
        return carry

    lax.fori_loop(0, lax.div(live + GANG - 1, GANG), gang, 0)

    ones = jnp.ones((16, 256), BF16)

    def near_out(owner, carry):
        boxed = held_ref.at[owner]
        for c in range(0, cap, 2):
            rows = []
            for n in (0, 1):
                rows.append(jnp.concatenate(halves(heat_acc[owner * cap + c + n]), 1))
            heats = lax.dot_general(
                ones, jnp.concatenate(rows, 0), (((1,), (1,)), ((), ())), preferred_element_type=F32
            )
            for n in (0, 1):
                slot = owner * cap + c + n
                sums = acc[slot]
                heat = jnp.sum(sums[16:24], 0, keepdims=True) + heats[0:1, 128 * n : 128 * n + 128]
                base = boxed[8 * (c + n) : 8 * (c + n) + 8] - MIDDLE
                out_ref[owner, 4 * (c + n) : 4 * (c + n) + 4] = result_rows(base, sums, heat)
        return carry

    def far_out(owner, carry):
        boxed = held_ref.at[n_tile + owner]
        for c in range(cap):
            sums = acc[slots + owner * cap + c]
            heat = jnp.sum(sums[16:24], 0, keepdims=True)
            base = boxed[8 * c : 8 * c + 8] - MIDDLE
            out_ref[n_tile + owner, 4 * c : 4 * c + 4] = result_rows(base, sums, heat)
        return carry

    lax.fori_loop(0, n_tile, near_out, 0)
    lax.fori_loop(0, n_tile, far_out, 0)


def pair_terms(n_tile, cap, pairs, live, held):
    slots = n_tile * cap
    smem = pl.BlockSpec(memory_space=pltpu.SMEM)
    vmem = pl.BlockSpec(memory_space=pltpu.VMEM)
    return pl.pallas_call(
        functools.partial(pair_kernel, n_tile, cap),
        out_shape=jax.ShapeDtypeStruct((2 * n_tile, 4 * cap, 128), F32),
        in_specs=[smem, smem, vmem],
        out_specs=vmem,
        scratch_shapes=[
            pltpu.VMEM((slots, 128, K_WIDE), BF16),
            pltpu.VMEM((2 * slots, K_WIDE, 256), BF16),
            pltpu.VMEM((2 * slots, K_SLIM, 256), BF16),
            pltpu.VMEM((2 * slots, 16, 128), BF16),
            pltpu.VMEM((slots, 128, 128), I32),
            pltpu.VMEM((2 * slots, 1, 128), I32),
            pltpu.VMEM((2 * slots + 1, 24, 128), F32),
            pltpu.VMEM((slots + 1, 128, 128), F32),
        ],
        compiler_params=pltpu.CompilerParams(vmem_limit_bytes=63 * MIB),
        name="pair_terms",
    )(pairs, live, held)


def return_kernel(n_grp, n_tile, terms_ref, got_ref, box, send_sems, recv_sems):
    g, t = lax.axis_index("grp"), lax.axis_index("tile")
    above, below = lax.rem(g + 1, n_grp), lax.rem(g + n_grp - 1, n_grp)
    barrier = pltpu.get_barrier_semaphore()
    for step in range(n_tile):
        owner = lax.rem(t + step, n_tile)
        if step:
            pl.semaphore_signal(barrier, inc=1, device_id=(g, owner), device_id_type=MESH)
        pl.semaphore_signal(barrier, inc=1, device_id=(above, owner), device_id_type=MESH)
    pl.semaphore_wait(barrier, 2 * n_tile - 1)

    def near(owner, slot):
        return pltpu.make_async_remote_copy(
            src_ref=terms_ref.at[owner], dst_ref=box.at[slot], send_sem=send_sems.at[owner], recv_sem=recv_sems.at[slot],
            device_id=(g, owner), device_id_type=MESH,
        )

    def far(owner, slot):
        return pltpu.make_async_remote_copy(
            src_ref=terms_ref.at[n_tile + owner], dst_ref=box.at[n_tile + slot], send_sem=send_sems.at[n_tile + owner],
            recv_sem=recv_sems.at[n_tile + slot], device_id=(below, owner), device_id_type=MESH,
        )

    def start(step, carry):
        owner = lax.rem(t + step, n_tile)
        far(owner, t).start()
        near(owner, t).start()
        return carry

    far(t, t).start()
    lax.fori_loop(1, n_tile, start, 0)
    box[t] = terms_ref[t]
    far(t, t).wait()

    def finish(step, carry):
        other = lax.rem(t + step, n_tile)
        far(other, other).wait_send()
        near(other, other).wait_send()
        far(other, other).wait_recv()
        near(other, other).wait_recv()
        return carry

    lax.fori_loop(1, n_tile, finish, 0)
    got_ref[...] = box[...]


def return_terms(n_grp, n_tile, terms):
    vmem = pl.BlockSpec(memory_space=pltpu.VMEM)
    sems = pltpu.SemaphoreType.DMA((2 * n_tile,))
    return pl.pallas_call(
        functools.partial(return_kernel, n_grp, n_tile),
        out_shape=jax.ShapeDtypeStruct(terms.shape, F32),
        in_specs=[vmem],
        out_specs=vmem,
        scratch_shapes=[pltpu.VMEM(terms.shape, F32), sems, sems],
        compiler_params=pltpu.CompilerParams(collective_id=1, has_side_effects=True, vmem_limit_bytes=24 * MIB),
        name="return_terms",
    )(terms)


def total_kernel(n_tile, cap, blocks, places_ref, got_ref, self_ref, out_ref, acc):
    acc[...] = self_ref[...]

    def add(worker, carry):
        for c in range(cap):
            place = places_ref[worker * cap + c]
            rows = slice(4 * c, 4 * c + 4)
            acc[place] += got_ref[worker, rows] + got_ref[n_tile + worker, rows]
        return carry

    lax.fori_loop(0, n_tile, add, 0)

    def put(b, carry):
        out_ref[:, pl.ds(pl.multiple_of(b * 128, 128), 128)] = acc[b]
        return carry

    lax.fori_loop(0, blocks, put, 0, unroll=8)


def total_terms(n_tile, cap, blocks, places, got, selfs):
    smem = pl.BlockSpec(memory_space=pltpu.SMEM)
    vmem = pl.BlockSpec(memory_space=pltpu.VMEM)
    return pl.pallas_call(
        functools.partial(total_kernel, n_tile, cap, blocks),
        out_shape=jax.ShapeDtypeStruct((4, blocks * 128), F32),
        in_specs=[smem, vmem, vmem],
        out_specs=vmem,
        scratch_shapes=[pltpu.VMEM((blocks, 4, 128), F32)],
        compiler_params=pltpu.CompilerParams(vmem_limit_bytes=24 * MIB),
        name="total_terms",
    )(places, got, selfs)


def per_device(
    molecule_coords,
    molecule_speeds,
    molecule_thermal_state,
    conservative_strength,
    noise_keys,
    exported_tile_places,
    tile_couplings,
    processor_coupling_tally,
):
    n_grp, n_tile = lax.axis_size("grp"), lax.axis_size("tile")
    blocks = molecule_coords.shape[1] // 128
    cap = exported_tile_places.shape[2]
    places = exported_tile_places.reshape(-1)
    beads = (
        molecule_coords,
        molecule_speeds,
        molecule_thermal_state.reshape(blocks, 128),
        conservative_strength.reshape(blocks, 128),
        noise_keys.reshape(blocks, 128),
    )
    pairs = jnp.pad(tile_couplings.reshape(-1), (0, 2 * GANG))
    held = gather_blocks(n_grp, n_tile, cap, blocks, places, *beads)
    selfs = self_terms(blocks, *beads)
    terms = pair_terms(n_tile, cap, pairs, processor_coupling_tally, held)
    got = return_terms(n_grp, n_tile, terms)
    return total_terms(n_tile, cap, blocks, places, got, selfs)


def solution(mesh):
    in_specs = (
        P(None, ("grp", "tile")),
        P(None, ("grp", "tile")),
        P(("grp", "tile")),
        P(("grp", "tile")),
        P(("grp", "tile")),
        P(("grp", "tile"), None, None),
        P(("grp", "tile"), None, None),
        P(("grp", "tile")),
    )
    out_specs = P(None, ("grp", "tile"))
    return jax.shard_map(per_device, mesh=mesh, in_specs=in_specs, out_specs=out_specs, check_vma=False)
```

```python
import functools

import jax
import jax.numpy as jnp
from jax import lax
from jax.experimental import pallas as pl
from jax.experimental.pallas import tpu as pltpu
from jax.sharding import PartitionSpec as P

friction = 0.45
noise_amp = 0.3
conductivity = 0.1
MODULUS = 65521
MIDDLE = 0.8

F32 = jnp.float32
BF16 = jnp.bfloat16
I32 = jnp.int32
MESH = pl.DeviceIdType.MESH
MIB = 2**20

HASH_UNIT = 2.0**32
FORCE_UNIT = 2.0 * noise_amp / HASH_UNIT
PULL = friction / FORCE_UNIT
HEAT_UNIT = 0.5 * friction / (PULL * PULL)
WARM = conductivity / HEAT_UNIT
STRENGTH = 0.5 / FORCE_UNIT
STRENGTH_SHIFT = -0.5 / MODULUS * HASH_UNIT

GROUP_ROWS = 8
K_WIDE = 64
K_SLIM = 32


def round_up(value, multiple):
    return (value + multiple - 1) // multiple * multiple


def parts_of(value):
    high = value.astype(BF16).astype(F32)
    rest = value - high
    middle = rest.astype(BF16).astype(F32)
    low = (rest - middle).astype(BF16).astype(F32)
    return high, middle, low


def bead_terms(raw):
    shape = raw.shape
    row = lax.broadcasted_iota(I32, shape, 1)
    position = row < 3
    scale = jnp.where(row < 6, 1.0, jnp.where(row == 6, WARM, STRENGTH)).astype(F32)
    shift = jnp.where(position, -MIDDLE, jnp.where(row == 7, STRENGTH_SHIFT, 0.0)).astype(F32)
    base = raw * scale + shift
    high, middle, low = parts_of(base)
    swapped = jnp.concatenate([base[:, 3:6], base[:, 0:3], jnp.zeros_like(base[:, 0:2])], 1)
    square = jnp.sum(jnp.where(position, base * base, 0.0), 1, keepdims=True) + 0.005
    cross = PULL * jnp.sum(jnp.where(position, base * swapped, 0.0), 1, keepdims=True)
    return row, base, (high, middle, low), swapped, parts_of(square), parts_of(cross)


def rows_of(row, values, first=0):
    out = jnp.zeros(row.shape, F32)
    for at, value in enumerate(values):
        out = jnp.where(row == first + at, value, out)
    return out


def tall_rows(terms):
    row, _, (high, middle, low), _, square, cross = terms
    ones = jnp.ones(row.shape, F32)
    own = rows_of(row, square + cross)
    return jnp.concatenate([high, middle, low, ones, high, high, middle, own], 1)


def wide_rows(terms):
    row, base, (high, middle, low), swapped, square, cross = terms
    near = [jnp.where(row < 3, -2.0 * part, 0.0) for part in (high, middle, low)]
    pull = parts_of(-PULL * swapped)
    one_square = jnp.where(row < 3, 1.0, 0.0).astype(F32)
    one_cross = jnp.where((row >= 3) & (row < 6), 1.0, 0.0).astype(F32)

    def stack(part, theirs, one):
        return jnp.concatenate([part[0]] * 3 + [theirs, part[1], part[2], part[1], one], 1)

    wide = jnp.concatenate(
        [stack(near, rows_of(row, square), one_square), stack(pull, rows_of(row, cross), one_cross)], 2
    )
    one_strength = jnp.where(row == 7, 1.0, 0.0).astype(F32)
    one_warm = jnp.where(row == 6, -1.0, 0.0).astype(F32)
    strengths = rows_of(row, [part[:, 7:8] for part in (high, middle, low)])
    warmths = rows_of(row, [part[:, 6:7] for part in (high, middle, low)])
    slim = jnp.concatenate(
        [
            jnp.concatenate([one_strength] * 3 + [strengths], 1),
            jnp.concatenate([one_warm] * 3 + [warmths], 1),
        ],
        2,
    )
    return wide.astype(BF16), slim.astype(BF16)


def weigh_rows(terms):
    row, _, (high, middle, low), _, _, _ = terms
    second = rows_of(row, [middle[:, at : at + 1] for at in range(3)] + [low[:, at : at + 1] for at in range(3)] + [1.0])
    return jnp.concatenate([high, second], 1).astype(BF16)


def hash_rows(keys):
    whole = int(HASH_UNIT) // MODULUS
    left = int(HASH_UNIT) - whole * MODULUS
    seed = keys + 1.0
    extra = jnp.floor(seed * (left / MODULUS) + 0.5)
    return seed.astype(I32), seed.astype(I32) * whole + extra.astype(I32)


def interactions(tall, wide, slim, seeds, factors):
    return finish(products(tall, wide, slim), seeds, factors)


def products(tall, wide, slim):
    first = jnp.dot(tall, wide, preferred_element_type=F32)
    second = jnp.dot(tall[:, :K_SLIM], slim, preferred_element_type=F32)
    return first, second


def finish(both, seeds, factors):
    first, second = both
    radius2, pull = first[:, :128], first[:, 128:]
    strength, warmth = second[:, :128], second[:, 128:]
    turned = seeds * factors + jnp.int32(-(2**31))
    lift = jnp.maximum(lax.rsqrt(radius2) - 1.0, 0.0)
    drag = lift * pull
    gain = lift * (strength + turned.astype(F32) - drag)
    viscous = drag * drag
    conduct = lift * lift * radius2 * warmth
    return gain, viscous + conduct, viscous - conduct


def halves(value):
    high = value.astype(BF16)
    return high, (value - high.astype(F32)).astype(BF16)


SELF_GANG = 4


def result_rows(base, sums, heat):
    moved = sums[0:3] + sums[8:11] + sums[11:14]
    force = FORCE_UNIT * (base[0:3] * sums[14:15] - moved)
    return jnp.concatenate([force, HEAT_UNIT * heat], 0)


def self_blocks(first, beads, out_ref, at):
    coords_ref, speeds_ref, temp_ref, strength_ref, keys_ref = beads
    raws, seeds, factors = [], [], []
    for n in range(SELF_GANG):
        b = first + n
        lanes = pl.ds(pl.multiple_of(b * 128, 128), 128)
        raws.append(
            jnp.concatenate(
                [coords_ref[:, lanes], speeds_ref[:, lanes], temp_ref[pl.ds(b, 1)], strength_ref[pl.ds(b, 1)]], 0
            )
        )
        seed, factor = hash_rows(keys_ref[pl.ds(b, 1)].astype(F32))
        seeds.append(seed)
        factors.append(factor)
    terms = bead_terms(jnp.stack(raws))
    wide, slim = wide_rows(terms)
    tall, weigh = tall_rows(terms), weigh_rows(terms)
    stacks = [
        jnp.concatenate([tall[n], jnp.broadcast_to(seeds[n].astype(F32), (64, 128))], 0).T for n in range(SELF_GANG)
    ]
    both = [products(stacks[n][:, :K_WIDE].astype(BF16), wide[n], slim[n]) for n in range(SELF_GANG)]
    halved, heats = [], []
    for n in range(SELF_GANG):
        mine = jnp.broadcast_to(stacks[n][:, K_WIDE : K_WIDE + 1].astype(I32), (128, 128))
        gain, _, heat = finish(both[n], mine, factors[n])
        halved.append(jnp.concatenate(halves(gain), 0))
        heats.append(jnp.sum(heat, 0, keepdims=True))
    for n in range(0, SELF_GANG, 2):
        left = jnp.concatenate([jnp.concatenate([weigh[m], weigh[m]], 1) for m in (n, n + 1)], 0)
        sums = jnp.dot(left, jnp.concatenate(halved[n : n + 2], 1), preferred_element_type=F32)
        for m in (0, 1):
            mine = sums[16 * m : 16 * m + 16, 128 * m : 128 * m + 128]
            out_ref[at + n + m] = result_rows(terms[1][n + m], mine, heats[n + m])


def gather_kernel(
    n_grp, n_tile, cap, blocks, places_ref, coords_hbm, speeds_hbm, temp_hbm, strength_hbm, keys_hbm,
    held_ref, self_ref, own, box, send_sems, recv_sems, up_sems, down_sems, home_sem, bead_sems, *beads,
):
    sources = (coords_hbm, speeds_hbm, temp_hbm, strength_hbm, keys_hbm)
    loads = [pltpu.make_async_copy(source, beads[n], bead_sems.at[n]) for n, source in enumerate(sources)]
    for load in loads:
        load.start()
    coords_ref, speeds_ref, temp_ref, strength_ref, keys_ref = beads
    g, t = lax.axis_index("grp"), lax.axis_index("tile")
    above, below = lax.rem(g + 1, n_grp), lax.rem(g + n_grp - 1, n_grp)
    barrier = pltpu.get_barrier_semaphore()
    for step in range(1, n_tile):
        pl.semaphore_signal(barrier, inc=1, device_id=(g, lax.rem(t + step, n_tile)), device_id_type=MESH)
    pl.semaphore_signal(barrier, inc=1, device_id=(below, t), device_id_type=MESH)

    for load in loads:
        load.wait()

    def pack(b, carry):
        lanes = pl.ds(pl.multiple_of(b * 128, 128), 128)
        own[b, 0:3] = coords_ref[:, lanes]
        own[b, 3:6] = speeds_ref[:, lanes]
        own[b, 6:7] = temp_ref[pl.ds(b, 1)]
        own[b, 7:8] = strength_ref[pl.ds(b, 1)]
        own[b, 8:9] = keys_ref[pl.ds(b, 1)].astype(F32)
        return carry

    lax.fori_loop(0, blocks, pack, 0, unroll=8)

    def fill(worker):
        for c in range(cap):
            place = places_ref[0, c, worker]
            box[worker, 8 * c : 8 * c + 8] = own[place, 0:8]
            box[worker, 8 * cap + c : 8 * cap + c + 1] = own[place, 8:9]

    def outgoing(step):
        worker = lax.rem(t + step, n_tile)
        return pltpu.make_async_remote_copy(
            src_ref=box.at[worker], dst_ref=held_ref.at[t], send_sem=send_sems.at[step], recv_sem=recv_sems.at[t],
            device_id=(g, worker), device_id_type=MESH,
        )

    def incoming(owner):
        return pltpu.make_async_remote_copy(
            src_ref=box.at[owner], dst_ref=held_ref.at[owner], send_sem=send_sems.at[0], recv_sem=recv_sems.at[owner],
            device_id=(g, owner), device_id_type=MESH,
        )

    def upward(owner, source):
        return pltpu.make_async_remote_copy(
            src_ref=source.at[owner], dst_ref=held_ref.at[n_tile + owner], send_sem=up_sems.at[owner], recv_sem=down_sems.at[owner],
            device_id=(above, t), device_id_type=MESH,
        )

    pl.semaphore_wait(barrier, n_tile)

    def send(step, carry):
        fill(lax.rem(t + step, n_tile))
        outgoing(step).start()
        return carry

    lax.fori_loop(1, n_tile, send, 0)
    fill(t)
    home = pltpu.make_async_copy(box.at[t], held_ref.at[t], home_sem)
    home.start()
    upward(t, box).start()

    def take(step, carry):
        owner = lax.rem(t + n_tile - step, n_tile)
        incoming(owner).wait_recv()
        upward(owner, held_ref).start()
        some = (step - 1) * SELF_GANG
        self_blocks(some, beads, self_ref, some)
        return carry

    lax.fori_loop(1, n_tile, take, 0)
    last = (n_tile - 1) * SELF_GANG
    self_blocks(last, beads, self_ref, last)
    home.wait()

    def finish(owner, carry):
        copy = upward(owner, held_ref)
        copy.wait_send()
        copy.wait_recv()
        return carry

    lax.fori_loop(0, n_tile, finish, 0)

    def sent(step, carry):
        outgoing(step).wait_send()
        return carry

    lax.fori_loop(1, n_tile, sent, 0)


def bead_buffers(blocks):
    wide, flat = pltpu.VMEM((3, blocks * 128), F32), pltpu.VMEM((blocks, 128), F32)
    return [wide, wide, flat, flat, pltpu.VMEM((blocks, 128), I32)]


def gather_blocks(n_grp, n_tile, cap, blocks, places, coords, speeds, temp, strength, keys):
    rows = round_up(9 * cap, 8)
    box = pltpu.VMEM((n_tile, rows, 128), F32)
    sems = pltpu.SemaphoreType.DMA((n_tile,))
    vmem = pl.BlockSpec(memory_space=pltpu.VMEM)
    hbm = pl.BlockSpec(memory_space=pltpu.HBM)
    return pl.pallas_call(
        functools.partial(gather_kernel, n_grp, n_tile, cap, blocks),
        out_shape=[
            jax.ShapeDtypeStruct((2 * n_tile, rows, 128), F32),
            jax.ShapeDtypeStruct((n_tile * SELF_GANG, 4, 128), F32),
        ],
        in_specs=[pl.BlockSpec(memory_space=pltpu.SMEM)] + [hbm] * 5,
        out_specs=[hbm, vmem],
        scratch_shapes=[
            pltpu.VMEM((blocks, 16, 128), F32), box, sems, sems, sems, sems, pltpu.SemaphoreType.DMA,
            pltpu.SemaphoreType.DMA((5,)),
            *bead_buffers(blocks),
        ],
        compiler_params=pltpu.CompilerParams(collective_id=0, has_side_effects=True, vmem_limit_bytes=63 * MIB),
        name="gather_blocks",
    )(places, coords, speeds, temp, strength, keys)


GANG = 16
AHEAD = 0
LAG = 6
LAG_AT = 0


def pair_kernel(
    n_tile, cap, pairs_ref, live_ref, held_hbm, out_ref,
    held_ref, held_sems, tall_s, wide_s, slim_s, weigh_s, seeds_s, factor_s, acc, heat_acc, *gains,
):
    slots = n_tile * cap

    def load(half):
        some = pl.ds(half * n_tile, n_tile)
        return pltpu.make_async_copy(held_hbm.at[some], held_ref.at[some], held_sems.at[half])

    load(0).start()
    load(1).start()

    def prepare(owner, first, with_tall):
        boxed = held_ref.at[owner]
        raw = boxed[0 : 8 * cap].reshape(cap, 8, 128)
        seed, factor = hash_rows(boxed[8 * cap : 9 * cap])
        for c in range(0, cap, 4):
            slot = first + c
            terms = bead_terms(raw[c : c + 4])
            wide, slim = wide_rows(terms)
            wide_s[pl.ds(slot, 4)] = wide
            slim_s[pl.ds(slot, 4)] = slim
            weigh_s[pl.ds(slot, 4)] = weigh_rows(terms)
            acc[pl.ds(slot, 4)] = jnp.zeros((4, 24, 128), F32)
            for n in range(4):
                factor_s[slot + n] = factor[c + n : c + n + 1]
            if with_tall:
                tall = tall_rows(terms)
                for n in range(4):
                    mine = jnp.broadcast_to(seed[c + n : c + n + 1].astype(F32), (64, 128))
                    stack = jnp.concatenate([tall[n], mine], 0).T
                    tall_s[slot + n] = stack[:, :K_WIDE].astype(BF16)
                    seeds_s[slot + n] = jnp.broadcast_to(stack[:, K_WIDE : K_WIDE + 1].astype(I32), (128, 128))
                    heat_acc[slot + n] = jnp.zeros((128, 128), F32)

    def near_step(owner, carry):
        prepare(owner, owner * cap, True)
        return carry

    def far_step(owner, carry):
        prepare(n_tile + owner, slots + owner * cap, False)
        return carry

    load(0).wait()
    lax.fori_loop(0, n_tile, near_step, 0)
    load(1).wait()
    lax.fori_loop(0, n_tile, far_step, 0)

    live = live_ref[0]

    def gang(step, carry):
        made = {}

        def place(u):
            k = step * GANG + u
            at = jnp.minimum(jnp.maximum(k, 0) if u < 0 else k, pairs_ref.shape[2] - 1)
            return pairs_ref[0, 0, at], pairs_ref[0, 1, at], ((k >= live) | (k < 0)) if u < 0 else (k >= live)

        def multiply(u):
            p, q, _ = place(u)
            made[u] = products(tall_s[p], wide_s[q], slim_s[q])

        def evaluate(u):
            p, q, dead = place(u)
            gain, heat_p, heat_q = finish(made.pop(u), seeds_s[p], factor_s[q])
            heat_acc[jnp.where(dead, slots, p)] += heat_p
            acc[jnp.where(dead, 2 * slots, q), 16:24] += jnp.sum(heat_q.reshape(16, 8, 128), 0)
            gains[u % GANG][0:128], gains[u % GANG][128:256] = halves(gain)

        def reduce(u):
            here = [place(v) for v in (u, u + 1)]
            first, second = gains[u % GANG], gains[(u + 1) % GANG]
            weigh_p = [weigh_s[p] for p, _, _ in here]
            weigh_q = [weigh_s[q] for _, q, _ in here]
            down = jnp.concatenate([first[...], second[...]], 1)
            across = jnp.concatenate(
                [jnp.concatenate([ref[0:128], ref[128:256]], 1) for ref in (first, second)], 0
            )
            left = jnp.concatenate([jnp.concatenate([w, w], 1) for w in weigh_p], 0)
            right = jnp.concatenate([jnp.concatenate([w, w], 1) for w in weigh_q], 0)
            on_q = jnp.dot(left, down, preferred_element_type=F32)
            on_p = lax.dot_general(right, across, (((1,), (1,)), ((), ())), preferred_element_type=F32)
            for v, (p, q, dead) in enumerate(here):
                rows, lanes = slice(16 * v, 16 * v + 16), slice(128 * v, 128 * v + 128)
                acc[jnp.where(dead, 2 * slots, p), 0:16] += on_p[rows, lanes]
                acc[jnp.where(dead, 2 * slots, q), 0:16] += on_q[rows, lanes]

        for u in range(-AHEAD, GANG):
            if 0 <= u + AHEAD < GANG:
                multiply(u + AHEAD)
            if u >= 0:
                evaluate(u)
                if u % 2 == LAG_AT:
                    reduce(u - LAG_AT - LAG)
        return carry

    lax.fori_loop(0, lax.div(live + LAG + GANG - 1, GANG), gang, 0)

    ones = jnp.ones((16, 256), BF16)

    def near_out(owner, carry):
        boxed = held_ref.at[owner]
        for c in range(0, cap, 2):
            rows = []
            for n in (0, 1):
                rows.append(jnp.concatenate(halves(heat_acc[owner * cap + c + n]), 1))
            heats = lax.dot_general(
                ones, jnp.concatenate(rows, 0), (((1,), (1,)), ((), ())), preferred_element_type=F32
            )
            for n in (0, 1):
                slot = owner * cap + c + n
                sums = acc[slot]
                heat = jnp.sum(sums[16:24], 0, keepdims=True) + heats[0:1, 128 * n : 128 * n + 128]
                base = boxed[8 * (c + n) : 8 * (c + n) + 8] - MIDDLE
                out_ref[owner, 4 * (c + n) : 4 * (c + n) + 4] = result_rows(base, sums, heat)
        return carry

    def far_out(owner, carry):
        boxed = held_ref.at[n_tile + owner]
        for c in range(cap):
            sums = acc[slots + owner * cap + c]
            heat = jnp.sum(sums[16:24], 0, keepdims=True)
            base = boxed[8 * c : 8 * c + 8] - MIDDLE
            out_ref[n_tile + owner, 4 * c : 4 * c + 4] = result_rows(base, sums, heat)
        return carry

    lax.fori_loop(0, n_tile, near_out, 0)
    lax.fori_loop(0, n_tile, far_out, 0)


def pair_terms(n_tile, cap, pairs, live, held):
    slots = n_tile * cap
    smem = pl.BlockSpec(memory_space=pltpu.SMEM)
    vmem = pl.BlockSpec(memory_space=pltpu.VMEM)
    hbm = pl.BlockSpec(memory_space=pltpu.HBM)
    return pl.pallas_call(
        functools.partial(pair_kernel, n_tile, cap),
        out_shape=jax.ShapeDtypeStruct((2 * n_tile, 4 * cap, 128), F32),
        in_specs=[smem, smem, hbm],
        out_specs=vmem,
        scratch_shapes=[
            pltpu.VMEM(held.shape, F32),
            pltpu.SemaphoreType.DMA((2,)),
            pltpu.VMEM((slots, 128, K_WIDE), BF16),
            pltpu.VMEM((2 * slots, K_WIDE, 256), BF16),
            pltpu.VMEM((2 * slots, K_SLIM, 256), BF16),
            pltpu.VMEM((2 * slots, 16, 128), BF16),
            pltpu.VMEM((slots, 128, 128), I32),
            pltpu.VMEM((2 * slots, 1, 128), I32),
            pltpu.VMEM((2 * slots + 1, 24, 128), F32),
            pltpu.VMEM((slots + 1, 128, 128), F32),
            *[pltpu.VMEM((256, 128), BF16)] * GANG,
        ],
        compiler_params=pltpu.CompilerParams(vmem_limit_bytes=63 * MIB),
        name="pair_terms",
    )(pairs, live, held)


def return_kernel(
    n_grp, n_tile, blocks, terms_ref, coords_hbm, speeds_hbm, temp_hbm, strength_hbm, keys_hbm,
    got_ref, self_ref, send_sems, recv_sems, home_sem, bead_sems, *beads,
):
    sources = (coords_hbm, speeds_hbm, temp_hbm, strength_hbm, keys_hbm)
    loads = [pltpu.make_async_copy(source, beads[n], bead_sems.at[n]) for n, source in enumerate(sources)]
    for load in loads:
        load.start()
    g, t = lax.axis_index("grp"), lax.axis_index("tile")
    above, below = lax.rem(g + 1, n_grp), lax.rem(g + n_grp - 1, n_grp)
    barrier = pltpu.get_barrier_semaphore()
    for step in range(n_tile):
        owner = lax.rem(t + step, n_tile)
        if step:
            pl.semaphore_signal(barrier, inc=1, device_id=(g, owner), device_id_type=MESH)
        pl.semaphore_signal(barrier, inc=1, device_id=(above, owner), device_id_type=MESH)
    pl.semaphore_wait(barrier, 2 * n_tile - 1)

    def near(owner, slot):
        return pltpu.make_async_remote_copy(
            src_ref=terms_ref.at[owner], dst_ref=got_ref.at[slot], send_sem=send_sems.at[owner], recv_sem=recv_sems.at[slot],
            device_id=(g, owner), device_id_type=MESH,
        )

    def far(owner, slot):
        return pltpu.make_async_remote_copy(
            src_ref=terms_ref.at[n_tile + owner], dst_ref=got_ref.at[n_tile + slot], send_sem=send_sems.at[n_tile + owner],
            recv_sem=recv_sems.at[n_tile + slot], device_id=(below, owner), device_id_type=MESH,
        )

    def start(step, carry):
        owner = lax.rem(t + step, n_tile)
        far(owner, t).start()
        near(owner, t).start()
        return carry

    far(t, t).start()
    lax.fori_loop(1, n_tile, start, 0)
    home = pltpu.make_async_copy(terms_ref.at[t], got_ref.at[t], home_sem)
    home.start()
    for load in loads:
        load.wait()
    done = n_tile * SELF_GANG

    def selfs(step, carry):
        self_blocks(done + step * SELF_GANG, beads, self_ref, step * SELF_GANG)
        return carry

    lax.fori_loop(0, (blocks - done) // SELF_GANG, selfs, 0)
    home.wait()
    far(t, t).wait()

    def finish(step, carry):
        other = lax.rem(t + step, n_tile)
        far(other, other).wait_send()
        near(other, other).wait_send()
        far(other, other).wait_recv()
        near(other, other).wait_recv()
        return carry

    lax.fori_loop(1, n_tile, finish, 0)


def return_terms(n_grp, n_tile, blocks, terms, beads):
    vmem = pl.BlockSpec(memory_space=pltpu.VMEM)
    hbm = pl.BlockSpec(memory_space=pltpu.HBM)
    sems = pltpu.SemaphoreType.DMA((2 * n_tile,))
    return pl.pallas_call(
        functools.partial(return_kernel, n_grp, n_tile, blocks),
        out_shape=[
            jax.ShapeDtypeStruct(terms.shape, F32),
            jax.ShapeDtypeStruct((blocks - n_tile * SELF_GANG, 4, 128), F32),
        ],
        in_specs=[hbm] * 6,
        out_specs=[vmem, vmem],
        scratch_shapes=[
            sems, sems, pltpu.SemaphoreType.DMA, pltpu.SemaphoreType.DMA((5,)),
            *bead_buffers(blocks),
        ],
        compiler_params=pltpu.CompilerParams(collective_id=1, has_side_effects=True, vmem_limit_bytes=63 * MIB),
        name="return_terms",
    )(terms, *beads)


def total_kernel(n_tile, cap, blocks, places_ref, got_ref, early_ref, late_ref, out_ref, acc):
    early = early_ref.shape[0]
    acc[0:early] = early_ref[...]
    acc[early:blocks] = late_ref[...]

    def add(worker, carry):
        for c in range(cap):
            place = places_ref[0, c, worker]
            rows = slice(4 * c, 4 * c + 4)
            acc[place] += got_ref[worker, rows] + got_ref[n_tile + worker, rows]
        return carry

    lax.fori_loop(0, n_tile, add, 0)

    def put(b, carry):
        out_ref[:, pl.ds(pl.multiple_of(b * 128, 128), 128)] = acc[b]
        return carry

    lax.fori_loop(0, blocks, put, 0, unroll=8)


def total_terms(n_tile, cap, blocks, places, got, early, late):
    smem = pl.BlockSpec(memory_space=pltpu.SMEM)
    vmem = pl.BlockSpec(memory_space=pltpu.VMEM)
    hbm = pl.BlockSpec(memory_space=pltpu.HBM)
    return pl.pallas_call(
        functools.partial(total_kernel, n_tile, cap, blocks),
        out_shape=jax.ShapeDtypeStruct((4, blocks * 128), F32),
        in_specs=[smem, vmem, vmem, vmem],
        out_specs=vmem,
        scratch_shapes=[pltpu.VMEM((blocks, 4, 128), F32)],
        compiler_params=pltpu.CompilerParams(vmem_limit_bytes=63 * MIB),
        name="total_terms",
    )(places, got, early, late)


def per_device(
    molecule_coords,
    molecule_speeds,
    molecule_thermal_state,
    conservative_strength,
    noise_keys,
    exported_tile_places,
    tile_couplings,
    processor_coupling_tally,
):
    n_grp, n_tile = lax.axis_size("grp"), lax.axis_size("tile")
    blocks = molecule_coords.shape[1] // 128
    cap = exported_tile_places.shape[2]
    places = exported_tile_places.transpose(0, 2, 1)
    beads = (
        molecule_coords,
        molecule_speeds,
        molecule_thermal_state.reshape(blocks, 128),
        conservative_strength.reshape(blocks, 128),
        noise_keys.reshape(blocks, 128),
    )
    pairs = tile_couplings.transpose(0, 2, 1)
    held, early = gather_blocks(n_grp, n_tile, cap, blocks, places, *beads)
    terms = pair_terms(n_tile, cap, pairs, processor_coupling_tally, held)
    got, late = return_terms(n_grp, n_tile, blocks, terms, beads)
    return total_terms(n_tile, cap, blocks, places, got, early, late)


def solution(mesh):
    in_specs = (
        P(None, ("grp", "tile")),
        P(None, ("grp", "tile")),
        P(("grp", "tile")),
        P(("grp", "tile")),
        P(("grp", "tile")),
        P(("grp", "tile"), None, None),
        P(("grp", "tile"), None, None),
        P(("grp", "tile")),
    )
    out_specs = P(None, ("grp", "tile"))
    return jax.shard_map(per_device, mesh=mesh, in_specs=in_specs, out_specs=out_specs, check_vma=False)
```

```python
import functools

import jax
import jax.numpy as jnp
from jax import lax
from jax.experimental import pallas as pl
from jax.experimental.pallas import tpu as pltpu
from jax.sharding import PartitionSpec as P

friction = 0.45
noise_amp = 0.3
conductivity = 0.1
MODULUS = 65521
MIDDLE = 0.8

F32 = jnp.float32
BF16 = jnp.bfloat16
I32 = jnp.int32
MESH = pl.DeviceIdType.MESH
MIB = 2**20

HASH_UNIT = 2.0**32
FORCE_UNIT = 2.0 * noise_amp / HASH_UNIT
PULL = friction / FORCE_UNIT
HEAT_UNIT = 0.5 * friction / (PULL * PULL)
WARM = conductivity / HEAT_UNIT
STRENGTH = 0.5 / FORCE_UNIT
STRENGTH_SHIFT = -0.5 / MODULUS * HASH_UNIT

GROUP_ROWS = 8
K_WIDE = 64
K_SLIM = 32


def round_up(value, multiple):
    return (value + multiple - 1) // multiple * multiple


def parts_of(value):
    high = value.astype(BF16).astype(F32)
    rest = value - high
    middle = rest.astype(BF16).astype(F32)
    low = (rest - middle).astype(BF16).astype(F32)
    return high, middle, low


def bead_terms(raw):
    shape = raw.shape
    row = lax.broadcasted_iota(I32, shape, 1)
    position = row < 3
    scale = jnp.where(row < 6, 1.0, jnp.where(row == 6, WARM, STRENGTH)).astype(F32)
    shift = jnp.where(position, -MIDDLE, jnp.where(row == 7, STRENGTH_SHIFT, 0.0)).astype(F32)
    base = raw * scale + shift
    high, middle, low = parts_of(base)
    swapped = jnp.concatenate([base[:, 3:6], base[:, 0:3], jnp.zeros_like(base[:, 0:2])], 1)
    square = jnp.sum(jnp.where(position, base * base, 0.0), 1, keepdims=True) + 0.005
    cross = PULL * jnp.sum(jnp.where(position, base * swapped, 0.0), 1, keepdims=True)
    return row, base, (high, middle, low), swapped, parts_of(square), parts_of(cross)


def rows_of(row, values, first=0):
    out = jnp.zeros(row.shape, F32)
    for at, value in enumerate(values):
        out = jnp.where(row == first + at, value, out)
    return out


def tall_rows(terms):
    row, _, (high, middle, low), _, square, cross = terms
    ones = jnp.ones(row.shape, F32)
    own = rows_of(row, square + cross)
    return jnp.concatenate([high, middle, low, ones, high, high, middle, own], 1)


def wide_rows(terms):
    row, base, (high, middle, low), swapped, square, cross = terms
    near = [jnp.where(row < 3, -2.0 * part, 0.0) for part in (high, middle, low)]
    pull = parts_of(-PULL * swapped)
    one_square = jnp.where(row < 3, 1.0, 0.0).astype(F32)
    one_cross = jnp.where((row >= 3) & (row < 6), 1.0, 0.0).astype(F32)

    def stack(part, theirs, one):
        return jnp.concatenate([part[0]] * 3 + [theirs, part[1], part[2], part[1], one], 1)

    wide = jnp.concatenate(
        [stack(near, rows_of(row, square), one_square), stack(pull, rows_of(row, cross), one_cross)], 2
    )
    one_strength = jnp.where(row == 7, 1.0, 0.0).astype(F32)
    one_warm = jnp.where(row == 6, -1.0, 0.0).astype(F32)
    strengths = rows_of(row, [part[:, 7:8] for part in (high, middle, low)])
    warmths = rows_of(row, [part[:, 6:7] for part in (high, middle, low)])
    slim = jnp.concatenate(
        [
            jnp.concatenate([one_strength] * 3 + [strengths], 1),
            jnp.concatenate([one_warm] * 3 + [warmths], 1),
        ],
        2,
    )
    return wide.astype(BF16), slim.astype(BF16)


def weigh_rows(terms):
    row, _, (high, middle, low), _, _, _ = terms
    second = rows_of(row, [middle[:, at : at + 1] for at in range(3)] + [low[:, at : at + 1] for at in range(3)] + [1.0])
    return jnp.concatenate([high, second], 1).astype(BF16)


def hash_rows(keys):
    whole = int(HASH_UNIT) // MODULUS
    left = int(HASH_UNIT) - whole * MODULUS
    seed = keys + 1.0
    extra = jnp.floor(seed * (left / MODULUS) + 0.5)
    return seed.astype(I32), seed.astype(I32) * whole + extra.astype(I32)


def interactions(tall, wide, slim, seeds, factors):
    return finish(products(tall, wide, slim), seeds, factors)


def products(tall, wide, slim):
    first = jnp.dot(tall, wide, preferred_element_type=F32)
    second = jnp.dot(tall[:, :K_SLIM], slim, preferred_element_type=F32)
    return first, second


def finish(both, seeds, factors):
    first, second = both
    radius2, pull = first[:, :128], first[:, 128:]
    strength, warmth = second[:, :128], second[:, 128:]
    turned = seeds * factors + jnp.int32(-(2**31))
    lift = jnp.maximum(lax.rsqrt(radius2) - 1.0, 0.0)
    drag = lift * pull
    gain = lift * (strength + turned.astype(F32) - drag)
    viscous = drag * drag
    conduct = lift * lift * radius2 * warmth
    return gain, viscous + conduct, viscous - conduct


def halves(value):
    high = value.astype(BF16)
    return high, (value - high.astype(F32)).astype(BF16)


def result_rows(base, sums, heat):
    moved = sums[0:3] + sums[8:11] + sums[11:14]
    force = FORCE_UNIT * (base[0:3] * sums[14:15] - moved)
    return jnp.concatenate([force, HEAT_UNIT * heat], 0)


def self_blocks(first, count, beads, out_ref):
    coords_ref, speeds_ref, temp_ref, strength_ref, keys_ref = beads
    raws, seeds, factors = [], [], []
    for n in range(count):
        b = first + n
        lanes = pl.ds(pl.multiple_of(b * 128, 128), 128)
        raws.append(
            jnp.concatenate(
                [coords_ref[:, lanes], speeds_ref[:, lanes], temp_ref[pl.ds(b, 1)], strength_ref[pl.ds(b, 1)]], 0
            )
        )
        seed, factor = hash_rows(keys_ref[pl.ds(b, 1)].astype(F32))
        seeds.append(seed)
        factors.append(factor)
    terms = bead_terms(jnp.stack(raws))
    wide, slim = wide_rows(terms)
    tall, weigh = tall_rows(terms), weigh_rows(terms)
    stacks = [
        jnp.concatenate([tall[n], jnp.broadcast_to(seeds[n].astype(F32), (64, 128))], 0).T for n in range(count)
    ]
    both = [products(stacks[n][:, :K_WIDE].astype(BF16), wide[n], slim[n]) for n in range(count)]
    halved, heats = [], []
    for n in range(count):
        mine = jnp.broadcast_to(stacks[n][:, K_WIDE : K_WIDE + 1].astype(I32), (128, 128))
        gain, _, heat = finish(both[n], mine, factors[n])
        halved.append(jnp.concatenate(halves(gain), 0))
        heats.append(jnp.sum(heat, 0, keepdims=True))
    for n in range(0, count, 2):
        left = jnp.concatenate([jnp.concatenate([weigh[m], weigh[m]], 1) for m in (n, n + 1)], 0)
        sums = jnp.dot(left, jnp.concatenate(halved[n : n + 2], 1), preferred_element_type=F32)
        for m in (0, 1):
            mine = sums[16 * m : 16 * m + 16, 128 * m : 128 * m + 128]
            out_ref[first + n + m] = result_rows(terms[1][n + m], mine, heats[n + m])


def gather_kernel(
    n_grp, n_tile, cap, blocks, places_ref, coords_hbm, speeds_hbm, temp_hbm, strength_hbm, keys_hbm,
    held_ref, self_ref, own, box, send_sems, recv_sems, up_sems, down_sems, home_sem, bead_sems, *beads,
):
    sources = (coords_hbm, speeds_hbm, temp_hbm, strength_hbm, keys_hbm)
    loads = [pltpu.make_async_copy(source, beads[n], bead_sems.at[n]) for n, source in enumerate(sources)]
    for load in loads:
        load.start()
    coords_ref, speeds_ref, temp_ref, strength_ref, keys_ref = beads
    g, t = lax.axis_index("grp"), lax.axis_index("tile")
    above, below = lax.rem(g + 1, n_grp), lax.rem(g + n_grp - 1, n_grp)
    barrier = pltpu.get_barrier_semaphore()
    for step in range(1, n_tile):
        pl.semaphore_signal(barrier, inc=1, device_id=(g, lax.rem(t + step, n_tile)), device_id_type=MESH)
    pl.semaphore_signal(barrier, inc=1, device_id=(below, t), device_id_type=MESH)

    for load in loads:
        load.wait()

    def pack(b, carry):
        lanes = pl.ds(pl.multiple_of(b * 128, 128), 128)
        own[b, 0:3] = coords_ref[:, lanes]
        own[b, 3:6] = speeds_ref[:, lanes]
        own[b, 6:7] = temp_ref[pl.ds(b, 1)]
        own[b, 7:8] = strength_ref[pl.ds(b, 1)]
        own[b, 8:9] = keys_ref[pl.ds(b, 1)].astype(F32)
        return carry

    lax.fori_loop(0, blocks, pack, 0, unroll=8)

    def fill(worker):
        for c in range(cap):
            place = places_ref[0, c, worker]
            box[worker, 8 * c : 8 * c + 8] = own[place, 0:8]
            box[worker, 8 * cap + c : 8 * cap + c + 1] = own[place, 8:9]

    def outgoing(step):
        worker = lax.rem(t + step, n_tile)
        return pltpu.make_async_remote_copy(
            src_ref=box.at[worker], dst_ref=held_ref.at[t], send_sem=send_sems.at[step], recv_sem=recv_sems.at[t],
            device_id=(g, worker), device_id_type=MESH,
        )

    def incoming(owner):
        return pltpu.make_async_remote_copy(
            src_ref=box.at[owner], dst_ref=held_ref.at[owner], send_sem=send_sems.at[0], recv_sem=recv_sems.at[owner],
            device_id=(g, owner), device_id_type=MESH,
        )

    def upward(owner, source):
        return pltpu.make_async_remote_copy(
            src_ref=source.at[owner], dst_ref=held_ref.at[n_tile + owner], send_sem=up_sems.at[owner], recv_sem=down_sems.at[owner],
            device_id=(above, t), device_id_type=MESH,
        )

    pl.semaphore_wait(barrier, n_tile)

    def send(step, carry):
        fill(lax.rem(t + step, n_tile))
        outgoing(step).start()
        return carry

    lax.fori_loop(1, n_tile, send, 0)
    fill(t)
    home = pltpu.make_async_copy(box.at[t], held_ref.at[t], home_sem)
    home.start()
    upward(t, box).start()

    share = blocks // n_tile

    def take(step, carry):
        owner = lax.rem(t + n_tile - step, n_tile)
        incoming(owner).wait_recv()
        upward(owner, held_ref).start()
        self_blocks((step - 1) * share, share, beads, self_ref)
        return carry

    lax.fori_loop(1, n_tile, take, 0)
    self_blocks((n_tile - 1) * share, share, beads, self_ref)
    home.wait()

    def finish(owner, carry):
        copy = upward(owner, held_ref)
        copy.wait_send()
        copy.wait_recv()
        return carry

    lax.fori_loop(0, n_tile, finish, 0)

    def sent(step, carry):
        outgoing(step).wait_send()
        return carry

    lax.fori_loop(1, n_tile, sent, 0)


def bead_buffers(blocks):
    wide, flat = pltpu.VMEM((3, blocks * 128), F32), pltpu.VMEM((blocks, 128), F32)
    return [wide, wide, flat, flat, pltpu.VMEM((blocks, 128), I32)]


def gather_blocks(n_grp, n_tile, cap, blocks, places, coords, speeds, temp, strength, keys):
    rows = round_up(9 * cap, 8)
    box = pltpu.VMEM((n_tile, rows, 128), F32)
    sems = pltpu.SemaphoreType.DMA((n_tile,))
    vmem = pl.BlockSpec(memory_space=pltpu.VMEM)
    hbm = pl.BlockSpec(memory_space=pltpu.HBM)
    return pl.pallas_call(
        functools.partial(gather_kernel, n_grp, n_tile, cap, blocks),
        out_shape=[
            jax.ShapeDtypeStruct((2 * n_tile, rows, 128), F32),
            jax.ShapeDtypeStruct((blocks, 4, 128), F32),
        ],
        in_specs=[pl.BlockSpec(memory_space=pltpu.SMEM)] + [hbm] * 5,
        out_specs=[hbm, vmem],
        scratch_shapes=[
            pltpu.VMEM((blocks, 16, 128), F32), box, sems, sems, sems, sems, pltpu.SemaphoreType.DMA,
            pltpu.SemaphoreType.DMA((5,)),
            *bead_buffers(blocks),
        ],
        compiler_params=pltpu.CompilerParams(collective_id=0, has_side_effects=True, vmem_limit_bytes=63 * MIB),
        name="gather_blocks",
    )(places, coords, speeds, temp, strength, keys)


GANG = 64
AHEAD = 0
LAG = 6
LAG_AT = 0
SETTLE_AT = 9


def pair_kernel(
    n_tile, cap, pairs_ref, live_ref, held_hbm, out_ref,
    held_ref, held_sems, tall_s, wide_s, slim_s, weigh_s, seeds_s, factor_s, acc, column_s, *gains,
):
    slots = n_tile * cap

    def load(half):
        some = pl.ds(half * n_tile, n_tile)
        return pltpu.make_async_copy(held_hbm.at[some], held_ref.at[some], held_sems.at[half])

    load(0).start()
    load(1).start()

    def prepare(owner, first, with_tall):
        boxed = held_ref.at[owner]
        raw = boxed[0 : 8 * cap].reshape(cap, 8, 128)
        seed, factor = hash_rows(boxed[8 * cap : 9 * cap])
        for c in range(0, cap, 4):
            slot = first + c
            terms = bead_terms(raw[c : c + 4])
            wide, slim = wide_rows(terms)
            wide_s[pl.ds(slot, 4)] = wide
            slim_s[pl.ds(slot, 4)] = slim
            weigh_s[pl.ds(slot, 4)] = weigh_rows(terms)
            acc[pl.ds(slot, 4)] = jnp.zeros((4, 24, 128), F32)
            for n in range(4):
                factor_s[slot + n] = factor[c + n : c + n + 1]
            if with_tall:
                tall = tall_rows(terms)
                for n in range(4):
                    mine = jnp.broadcast_to(seed[c + n : c + n + 1].astype(F32), (64, 128))
                    stack = jnp.concatenate([tall[n], mine], 0).T
                    tall_s[slot + n] = stack[:, :K_WIDE].astype(BF16)
                    seeds_s[slot + n] = jnp.broadcast_to(stack[:, K_WIDE : K_WIDE + 1].astype(I32), (128, 128))

    def near_step(owner, carry):
        prepare(owner, owner * cap, True)
        return carry

    def far_step(owner, carry):
        prepare(n_tile + owner, slots + owner * cap, False)
        return carry

    load(0).wait()
    lax.fori_loop(0, n_tile, near_step, 0)
    load(1).wait()
    lax.fori_loop(0, n_tile, far_step, 0)

    live = live_ref[0]
    column_s[...] = jnp.zeros((128, 128), F32)

    def gang(step, carry, whole=True):
        made, columns = {}, []

        def place(u):
            k = step * GANG + u
            at = jnp.minimum(jnp.maximum(k, 0) if u < 0 else k, pairs_ref.shape[2] - 1)
            return pairs_ref[0, 0, at], pairs_ref[0, 1, at], ((k >= live) | (k < 0)) if u < 0 else (k >= live)

        def multiply(u):
            p, q, _ = place(u)
            made[u] = products(tall_s[p], wide_s[q], slim_s[q])

        def evaluate(u):
            p, q, dead = place(u)
            gain, heat_p, heat_q = finish(made.pop(u), seeds_s[p], factor_s[q])
            columns.append(jnp.sum(heat_p, 1, keepdims=True))
            acc[jnp.where(dead, 2 * slots, q), 16:24] += jnp.sum(heat_q.reshape(16, 8, 128), 0)
            gains[u % GANG][0:128], gains[u % GANG][128:256] = halves(gain)

        def reduce(u):
            here = [place(v) for v in (u, u + 1)]
            first, second = gains[u % GANG], gains[(u + 1) % GANG]
            weigh_p = [weigh_s[p] for p, _, _ in here]
            weigh_q = [weigh_s[q] for _, q, _ in here]
            down = jnp.concatenate([first[...], second[...]], 1)
            across = jnp.concatenate(
                [jnp.concatenate([ref[0:128], ref[128:256]], 1) for ref in (first, second)], 0
            )
            left = jnp.concatenate([jnp.concatenate([w, w], 1) for w in weigh_p], 0)
            right = jnp.concatenate([jnp.concatenate([w, w], 1) for w in weigh_q], 0)
            on_q = jnp.dot(left, down, preferred_element_type=F32)
            on_p = lax.dot_general(right, across, (((1,), (1,)), ((), ())), preferred_element_type=F32)
            for v, (p, q, dead) in enumerate(here):
                rows, lanes = slice(16 * v, 16 * v + 16), slice(128 * v, 128 * v + 128)
                acc[jnp.where(dead, 2 * slots, p), 0:16] += on_p[rows, lanes]
                acc[jnp.where(dead, 2 * slots, q), 0:16] += on_q[rows, lanes]

        def settle():
            rows = column_s[...].T
            for u in range(GANG):
                p, _, dead = place(u - GANG)
                acc[jnp.where(dead, 2 * slots, p), 16:17] += rows[u : u + 1]

        if not whole:
            for u in range(0, LAG, 2):
                reduce(u - LAG)
            settle()
            return carry

        for u in range(-AHEAD, GANG):
            if 0 <= u + AHEAD < GANG:
                multiply(u + AHEAD)
            if u >= 0:
                evaluate(u)
                if u % 2 == LAG_AT:
                    reduce(u - LAG_AT - LAG)
                if u == SETTLE_AT:
                    settle()
        column_s[:, 0:GANG] = jnp.concatenate(columns, 1)
        return carry

    gangs = lax.div(live + GANG - 1, GANG)
    lax.fori_loop(0, gangs, gang, 0)
    gang(gangs, 0, False)

    def near_out(owner, carry):
        boxed = held_ref.at[owner]
        for c in range(cap):
            sums = acc[owner * cap + c]
            heat = jnp.sum(sums[16:24], 0, keepdims=True)
            base = boxed[8 * c : 8 * c + 8] - MIDDLE
            out_ref[owner, 4 * c : 4 * c + 4] = result_rows(base, sums, heat)
        return carry

    def far_out(owner, carry):
        boxed = held_ref.at[n_tile + owner]
        for c in range(cap):
            sums = acc[slots + owner * cap + c]
            heat = jnp.sum(sums[16:24], 0, keepdims=True)
            base = boxed[8 * c : 8 * c + 8] - MIDDLE
            out_ref[n_tile + owner, 4 * c : 4 * c + 4] = result_rows(base, sums, heat)
        return carry

    lax.fori_loop(0, n_tile, near_out, 0)
    lax.fori_loop(0, n_tile, far_out, 0)


def pair_terms(n_tile, cap, pairs, live, held):
    slots = n_tile * cap
    smem = pl.BlockSpec(memory_space=pltpu.SMEM)
    vmem = pl.BlockSpec(memory_space=pltpu.VMEM)
    hbm = pl.BlockSpec(memory_space=pltpu.HBM)
    return pl.pallas_call(
        functools.partial(pair_kernel, n_tile, cap),
        out_shape=jax.ShapeDtypeStruct((2 * n_tile, 4 * cap, 128), F32),
        in_specs=[smem, smem, hbm],
        out_specs=vmem,
        scratch_shapes=[
            pltpu.VMEM(held.shape, F32),
            pltpu.SemaphoreType.DMA((2,)),
            pltpu.VMEM((slots, 128, K_WIDE), BF16),
            pltpu.VMEM((2 * slots, K_WIDE, 256), BF16),
            pltpu.VMEM((2 * slots, K_SLIM, 256), BF16),
            pltpu.VMEM((2 * slots, 16, 128), BF16),
            pltpu.VMEM((slots, 128, 128), I32),
            pltpu.VMEM((2 * slots, 1, 128), I32),
            pltpu.VMEM((2 * slots + 1, 24, 128), F32),
            pltpu.VMEM((128, 128), F32),
            *[pltpu.VMEM((256, 128), BF16)] * GANG,
        ],
        compiler_params=pltpu.CompilerParams(vmem_limit_bytes=63 * MIB),
        name="pair_terms",
    )(pairs, live, held)


def return_kernel(
    n_grp, n_tile, terms_ref, got_ref, send_sems, recv_sems, home_sem,
):
    g, t = lax.axis_index("grp"), lax.axis_index("tile")
    above, below = lax.rem(g + 1, n_grp), lax.rem(g + n_grp - 1, n_grp)
    barrier = pltpu.get_barrier_semaphore()
    for step in range(n_tile):
        owner = lax.rem(t + step, n_tile)
        if step:
            pl.semaphore_signal(barrier, inc=1, device_id=(g, owner), device_id_type=MESH)
        pl.semaphore_signal(barrier, inc=1, device_id=(above, owner), device_id_type=MESH)
    pl.semaphore_wait(barrier, 2 * n_tile - 1)

    def near(owner, slot):
        return pltpu.make_async_remote_copy(
            src_ref=terms_ref.at[owner], dst_ref=got_ref.at[slot], send_sem=send_sems.at[owner], recv_sem=recv_sems.at[slot],
            device_id=(g, owner), device_id_type=MESH,
        )

    def far(owner, slot):
        return pltpu.make_async_remote_copy(
            src_ref=terms_ref.at[n_tile + owner], dst_ref=got_ref.at[n_tile + slot], send_sem=send_sems.at[n_tile + owner],
            recv_sem=recv_sems.at[n_tile + slot], device_id=(below, owner), device_id_type=MESH,
        )

    def start(step, carry):
        owner = lax.rem(t + step, n_tile)
        far(owner, t).start()
        near(owner, t).start()
        return carry

    far(t, t).start()
    lax.fori_loop(1, n_tile, start, 0)
    home = pltpu.make_async_copy(terms_ref.at[t], got_ref.at[t], home_sem)
    home.start()
    home.wait()
    far(t, t).wait()

    def finish(step, carry):
        other = lax.rem(t + step, n_tile)
        far(other, other).wait_send()
        near(other, other).wait_send()
        far(other, other).wait_recv()
        near(other, other).wait_recv()
        return carry

    lax.fori_loop(1, n_tile, finish, 0)


def return_terms(n_grp, n_tile, terms):
    vmem = pl.BlockSpec(memory_space=pltpu.VMEM)
    hbm = pl.BlockSpec(memory_space=pltpu.HBM)
    sems = pltpu.SemaphoreType.DMA((2 * n_tile,))
    return pl.pallas_call(
        functools.partial(return_kernel, n_grp, n_tile),
        out_shape=jax.ShapeDtypeStruct(terms.shape, F32),
        in_specs=[hbm],
        out_specs=vmem,
        scratch_shapes=[sems, sems, pltpu.SemaphoreType.DMA],
        compiler_params=pltpu.CompilerParams(collective_id=1, has_side_effects=True, vmem_limit_bytes=63 * MIB),
        name="return_terms",
    )(terms)


def total_kernel(n_tile, cap, blocks, places_ref, got_ref, self_ref, out_ref, acc):
    acc[...] = self_ref[...]

    def add(worker, carry):
        for c in range(cap):
            place = places_ref[0, c, worker]
            rows = slice(4 * c, 4 * c + 4)
            acc[place] += got_ref[worker, rows] + got_ref[n_tile + worker, rows]
        return carry

    lax.fori_loop(0, n_tile, add, 0)

    def put(b, carry):
        out_ref[:, pl.ds(pl.multiple_of(b * 128, 128), 128)] = acc[b]
        return carry

    lax.fori_loop(0, blocks, put, 0, unroll=8)


def total_terms(n_tile, cap, blocks, places, got, selfs):
    smem = pl.BlockSpec(memory_space=pltpu.SMEM)
    vmem = pl.BlockSpec(memory_space=pltpu.VMEM)
    hbm = pl.BlockSpec(memory_space=pltpu.HBM)
    return pl.pallas_call(
        functools.partial(total_kernel, n_tile, cap, blocks),
        out_shape=jax.ShapeDtypeStruct((4, blocks * 128), F32),
        in_specs=[smem, vmem, vmem],
        out_specs=vmem,
        scratch_shapes=[pltpu.VMEM((blocks, 4, 128), F32)],
        compiler_params=pltpu.CompilerParams(vmem_limit_bytes=63 * MIB),
        name="total_terms",
    )(places, got, selfs)


def per_device(
    molecule_coords,
    molecule_speeds,
    molecule_thermal_state,
    conservative_strength,
    noise_keys,
    exported_tile_places,
    tile_couplings,
    processor_coupling_tally,
):
    n_grp, n_tile = lax.axis_size("grp"), lax.axis_size("tile")
    blocks = molecule_coords.shape[1] // 128
    cap = exported_tile_places.shape[2]
    places = exported_tile_places.transpose(0, 2, 1)
    beads = (
        molecule_coords,
        molecule_speeds,
        molecule_thermal_state.reshape(blocks, 128),
        conservative_strength.reshape(blocks, 128),
        noise_keys.reshape(blocks, 128),
    )
    pairs = tile_couplings.transpose(0, 2, 1)
    held, selfs = gather_blocks(n_grp, n_tile, cap, blocks, places, *beads)
    terms = pair_terms(n_tile, cap, pairs, processor_coupling_tally, held)
    got = return_terms(n_grp, n_tile, terms)
    return total_terms(n_tile, cap, blocks, places, got, selfs)


def solution(mesh):
    in_specs = (
        P(None, ("grp", "tile")),
        P(None, ("grp", "tile")),
        P(("grp", "tile")),
        P(("grp", "tile")),
        P(("grp", "tile")),
        P(("grp", "tile"), None, None),
        P(("grp", "tile"), None, None),
        P(("grp", "tile")),
    )
    out_specs = P(None, ("grp", "tile"))
    return jax.shard_map(per_device, mesh=mesh, in_specs=in_specs, out_specs=out_specs, check_vma=False)
```

```python
import functools

import jax
import jax.numpy as jnp
from jax import lax
from jax.experimental import pallas as pl
from jax.experimental.pallas import tpu as pltpu
from jax.sharding import PartitionSpec as P

friction = 0.45
noise_amp = 0.3
conductivity = 0.1
MODULUS = 65521
MIDDLE = 0.8

F32 = jnp.float32
BF16 = jnp.bfloat16
I32 = jnp.int32
MESH = pl.DeviceIdType.MESH
MIB = 2**20

HASH_UNIT = 2.0**32
FORCE_UNIT = 2.0 * noise_amp / HASH_UNIT
PULL = friction / FORCE_UNIT
HEAT_UNIT = 0.5 * friction / (PULL * PULL)
WARM = conductivity / HEAT_UNIT
STRENGTH = 0.5 / FORCE_UNIT
STRENGTH_SHIFT = -0.5 / MODULUS * HASH_UNIT

GROUP_ROWS = 8
K_WIDE = 64
K_SLIM = 32


def round_up(value, multiple):
    return (value + multiple - 1) // multiple * multiple


def parts_of(value):
    high = value.astype(BF16).astype(F32)
    rest = value - high
    middle = rest.astype(BF16).astype(F32)
    low = (rest - middle).astype(BF16).astype(F32)
    return high, middle, low


def bead_terms(raw):
    shape = raw.shape
    row = lax.broadcasted_iota(I32, shape, 1)
    position = row < 3
    scale = jnp.where(row < 6, 1.0, jnp.where(row == 6, WARM, STRENGTH)).astype(F32)
    shift = jnp.where(position, -MIDDLE, jnp.where(row == 7, STRENGTH_SHIFT, 0.0)).astype(F32)
    base = raw * scale + shift
    high, middle, low = parts_of(base)
    swapped = jnp.concatenate([base[:, 3:6], base[:, 0:3], jnp.zeros_like(base[:, 0:2])], 1)
    square = jnp.sum(jnp.where(position, base * base, 0.0), 1, keepdims=True) + 0.005
    cross = PULL * jnp.sum(jnp.where(position, base * swapped, 0.0), 1, keepdims=True)
    return row, base, (high, middle, low), swapped, parts_of(square), parts_of(cross)


def rows_of(row, values, first=0):
    out = jnp.zeros(row.shape, F32)
    for at, value in enumerate(values):
        out = jnp.where(row == first + at, value, out)
    return out


def tall_rows(terms):
    row, _, (high, middle, low), _, square, cross = terms
    ones = jnp.ones(row.shape, F32)
    own = rows_of(row, square + cross)
    return jnp.concatenate([high, middle, low, ones, high, high, middle, own], 1)


def wide_rows(terms):
    row, base, (high, middle, low), swapped, square, cross = terms
    near = [jnp.where(row < 3, -2.0 * part, 0.0) for part in (high, middle, low)]
    pull = parts_of(-PULL * swapped)
    one_square = jnp.where(row < 3, 1.0, 0.0).astype(F32)
    one_cross = jnp.where((row >= 3) & (row < 6), 1.0, 0.0).astype(F32)

    def stack(part, theirs, one):
        return jnp.concatenate([part[0]] * 3 + [theirs, part[1], part[2], part[1], one], 1)

    wide = jnp.concatenate(
        [stack(near, rows_of(row, square), one_square), stack(pull, rows_of(row, cross), one_cross)], 2
    )
    one_strength = jnp.where(row == 7, 1.0, 0.0).astype(F32)
    one_warm = jnp.where(row == 6, -1.0, 0.0).astype(F32)
    strengths = rows_of(row, [part[:, 7:8] for part in (high, middle, low)])
    warmths = rows_of(row, [part[:, 6:7] for part in (high, middle, low)])
    slim = jnp.concatenate(
        [
            jnp.concatenate([one_strength] * 3 + [strengths], 1),
            jnp.concatenate([one_warm] * 3 + [warmths], 1),
        ],
        2,
    )
    return wide.astype(BF16), slim.astype(BF16)


def weigh_rows(terms):
    row, _, (high, middle, low), _, _, _ = terms
    second = rows_of(row, [middle[:, at : at + 1] for at in range(3)] + [low[:, at : at + 1] for at in range(3)] + [1.0])
    return jnp.concatenate([high, second], 1).astype(BF16)


def hash_rows(keys):
    whole = int(HASH_UNIT) // MODULUS
    left = int(HASH_UNIT) - whole * MODULUS
    seed = keys + 1.0
    extra = jnp.floor(seed * (left / MODULUS) + 0.5)
    return seed.astype(I32), seed.astype(I32) * whole + extra.astype(I32)


def interactions(tall, wide, slim, seeds, factors):
    return finish(products(tall, wide, slim), seeds, factors)


def products(tall, wide, slim):
    first = jnp.dot(tall, wide, preferred_element_type=F32)
    second = jnp.dot(tall[:, :K_SLIM], slim, preferred_element_type=F32)
    return first, second


def finish(both, seeds, factors):
    first, second = both
    radius2, pull = first[:, :128], first[:, 128:]
    strength, warmth = second[:, :128], second[:, 128:]
    turned = seeds * factors + jnp.int32(-(2**31))
    lift = jnp.maximum(lax.rsqrt(radius2) - 1.0, 0.0)
    drag = lift * pull
    gain = lift * (strength + turned.astype(F32) - drag)
    viscous = drag * drag
    conduct = lift * lift * radius2 * warmth
    return gain, viscous + conduct, viscous - conduct


def halves(value):
    high = value.astype(BF16)
    return high, (value - high.astype(F32)).astype(BF16)


def result_rows(base, sums, heat):
    moved = sums[0:3] + sums[8:11] + sums[11:14]
    force = FORCE_UNIT * (base[0:3] * sums[14:15] - moved)
    return jnp.concatenate([force, HEAT_UNIT * heat], 0)


def self_blocks(first, count, beads, out_ref):
    coords_ref, speeds_ref, temp_ref, strength_ref, keys_ref = beads
    raws, seeds, factors = [], [], []
    for n in range(count):
        b = first + n
        lanes = pl.ds(pl.multiple_of(b * 128, 128), 128)
        raws.append(
            jnp.concatenate(
                [coords_ref[:, lanes], speeds_ref[:, lanes], temp_ref[pl.ds(b, 1)], strength_ref[pl.ds(b, 1)]], 0
            )
        )
        seed, factor = hash_rows(keys_ref[pl.ds(b, 1)].astype(F32))
        seeds.append(seed)
        factors.append(factor)
    terms = bead_terms(jnp.stack(raws))
    wide, slim = wide_rows(terms)
    tall, weigh = tall_rows(terms), weigh_rows(terms)
    stacks = [
        jnp.concatenate([tall[n], jnp.broadcast_to(seeds[n].astype(F32), (64, 128))], 0).T for n in range(count)
    ]
    both = [products(stacks[n][:, :K_WIDE].astype(BF16), wide[n], slim[n]) for n in range(count)]
    halved, heats = [], []
    for n in range(count):
        mine = jnp.broadcast_to(stacks[n][:, K_WIDE : K_WIDE + 1].astype(I32), (128, 128))
        gain, _, heat = finish(both[n], mine, factors[n])
        halved.append(jnp.concatenate(halves(gain), 0))
        heats.append(jnp.sum(heat, 0, keepdims=True))
    for n in range(0, count, 2):
        left = jnp.concatenate([jnp.concatenate([weigh[m], weigh[m]], 1) for m in (n, n + 1)], 0)
        sums = jnp.dot(left, jnp.concatenate(halved[n : n + 2], 1), preferred_element_type=F32)
        for m in (0, 1):
            mine = sums[16 * m : 16 * m + 16, 128 * m : 128 * m + 128]
            out_ref[first + n + m] = result_rows(terms[1][n + m], mine, heats[n + m])


def gather_kernel(
    n_grp, n_tile, cap, blocks, places_ref, coords_hbm, speeds_hbm, temp_hbm, strength_hbm, keys_hbm,
    held_ref, self_ref, own, box, send_sems, recv_sems, up_sems, down_sems, home_sem, bead_sems, *beads,
):
    sources = (coords_hbm, speeds_hbm, temp_hbm, strength_hbm, keys_hbm)
    loads = [pltpu.make_async_copy(source, beads[n], bead_sems.at[n]) for n, source in enumerate(sources)]
    for load in loads:
        load.start()
    coords_ref, speeds_ref, temp_ref, strength_ref, keys_ref = beads
    g, t = lax.axis_index("grp"), lax.axis_index("tile")
    above, below = lax.rem(g + 1, n_grp), lax.rem(g + n_grp - 1, n_grp)
    barrier = pltpu.get_barrier_semaphore()
    for step in range(1, n_tile):
        pl.semaphore_signal(barrier, inc=1, device_id=(g, lax.rem(t + step, n_tile)), device_id_type=MESH)
    pl.semaphore_signal(barrier, inc=1, device_id=(below, t), device_id_type=MESH)

    for load in loads:
        load.wait()

    def pack(b, carry):
        lanes = pl.ds(pl.multiple_of(b * 128, 128), 128)
        own[b, 0:3] = coords_ref[:, lanes]
        own[b, 3:6] = speeds_ref[:, lanes]
        own[b, 6:7] = temp_ref[pl.ds(b, 1)]
        own[b, 7:8] = strength_ref[pl.ds(b, 1)]
        own[b, 8:9] = keys_ref[pl.ds(b, 1)].astype(F32)
        return carry

    lax.fori_loop(0, blocks, pack, 0, unroll=8)

    def fill(worker):
        for c in range(cap):
            place = places_ref[c, 0, worker]
            box[worker, 8 * c : 8 * c + 8] = own[place, 0:8]
            box[worker, 8 * cap + c : 8 * cap + c + 1] = own[place, 8:9]

    def outgoing(step):
        worker = lax.rem(t + step, n_tile)
        return pltpu.make_async_remote_copy(
            src_ref=box.at[worker], dst_ref=held_ref.at[t], send_sem=send_sems.at[step], recv_sem=recv_sems.at[t],
            device_id=(g, worker), device_id_type=MESH,
        )

    def incoming(owner):
        return pltpu.make_async_remote_copy(
            src_ref=box.at[owner], dst_ref=held_ref.at[owner], send_sem=send_sems.at[0], recv_sem=recv_sems.at[owner],
            device_id=(g, owner), device_id_type=MESH,
        )

    def upward(owner, source):
        return pltpu.make_async_remote_copy(
            src_ref=source.at[owner], dst_ref=held_ref.at[n_tile + owner], send_sem=up_sems.at[owner], recv_sem=down_sems.at[owner],
            device_id=(above, t), device_id_type=MESH,
        )

    pl.semaphore_wait(barrier, n_tile)

    def send(step, carry):
        fill(lax.rem(t + step, n_tile))
        outgoing(step).start()
        return carry

    lax.fori_loop(1, n_tile, send, 0)
    fill(t)
    home = pltpu.make_async_copy(box.at[t], held_ref.at[t], home_sem)
    home.start()
    upward(t, box).start()

    share = blocks // n_tile

    def take(step, carry):
        owner = lax.rem(t + n_tile - step, n_tile)
        incoming(owner).wait_recv()
        upward(owner, held_ref).start()
        return carry

    def share_of(part, carry):
        self_blocks(part * share, share, beads, self_ref)
        return carry

    def take_beside(step, carry):
        take(step, carry)
        return share_of(EARLY + step - 1, carry)

    lax.fori_loop(0, EARLY, share_of, 0)
    lax.fori_loop(1, BESIDE + 1, take_beside, 0)
    lax.fori_loop(BESIDE + 1, n_tile, take, 0)
    lax.fori_loop(EARLY + BESIDE, n_tile, share_of, 0)
    home.wait()

    def finish(owner, carry):
        copy = upward(owner, held_ref)
        copy.wait_send()
        copy.wait_recv()
        return carry

    lax.fori_loop(0, n_tile, finish, 0)

    def sent(step, carry):
        outgoing(step).wait_send()
        return carry

    lax.fori_loop(1, n_tile, sent, 0)


def bead_buffers(blocks):
    wide, flat = pltpu.VMEM((3, blocks * 128), F32), pltpu.VMEM((blocks, 128), F32)
    return [wide, wide, flat, flat, pltpu.VMEM((blocks, 128), I32)]


def gather_blocks(n_grp, n_tile, cap, blocks, places, coords, speeds, temp, strength, keys):
    rows = round_up(9 * cap, 8)
    box = pltpu.VMEM((n_tile, rows, 128), F32)
    sems = pltpu.SemaphoreType.DMA((n_tile,))
    vmem = pl.BlockSpec(memory_space=pltpu.VMEM)
    hbm = pl.BlockSpec(memory_space=pltpu.HBM)
    return pl.pallas_call(
        functools.partial(gather_kernel, n_grp, n_tile, cap, blocks),
        out_shape=[
            jax.ShapeDtypeStruct((2 * n_tile, rows, 128), F32),
            jax.ShapeDtypeStruct((blocks, 4, 128), F32),
        ],
        in_specs=[pl.BlockSpec(memory_space=pltpu.SMEM)] + [hbm] * 5,
        out_specs=[hbm, vmem],
        scratch_shapes=[
            pltpu.VMEM((blocks, 16, 128), F32), box, sems, sems, sems, sems, pltpu.SemaphoreType.DMA,
            pltpu.SemaphoreType.DMA((5,)),
            *bead_buffers(blocks),
        ],
        compiler_params=pltpu.CompilerParams(collective_id=0, has_side_effects=True, vmem_limit_bytes=63 * MIB),
        name="gather_blocks",
    )(places, coords, speeds, temp, strength, keys)


GANG = 64
EARLY = 3
BESIDE = 6
AHEAD = 0
LAG = 6
LAG_AT = 0
SETTLE_AT = 9


def pair_kernel(
    n_tile, cap, pairs_ref, live_ref, held_hbm, out_ref,
    held_ref, held_sems, tall_s, wide_s, slim_s, weigh_s, seeds_s, factor_s, acc, column_s, *gains,
):
    slots = n_tile * cap

    def load(half):
        some = pl.ds(half * n_tile, n_tile)
        return pltpu.make_async_copy(held_hbm.at[some], held_ref.at[some], held_sems.at[half])

    load(0).start()
    load(1).start()

    def prepare(owner, first, with_tall):
        boxed = held_ref.at[owner]
        raw = boxed[0 : 8 * cap].reshape(cap, 8, 128)
        seed, factor = hash_rows(boxed[8 * cap : 9 * cap])
        for c in range(0, cap, 4):
            slot = first + c
            terms = bead_terms(raw[c : c + 4])
            wide, slim = wide_rows(terms)
            wide_s[pl.ds(slot, 4)] = wide
            slim_s[pl.ds(slot, 4)] = slim
            weigh_s[pl.ds(slot, 4)] = weigh_rows(terms)
            acc[pl.ds(slot, 4)] = jnp.zeros((4, 24, 128), F32)
            for n in range(4):
                factor_s[slot + n] = factor[c + n : c + n + 1]
            if with_tall:
                tall = tall_rows(terms)
                for n in range(4):
                    mine = jnp.broadcast_to(seed[c + n : c + n + 1], (128, 128))
                    tall_s[slot + n] = tall[n].astype(BF16).T
                    seeds_s[slot + n] = mine.T

    def near_step(owner, carry):
        prepare(owner, owner * cap, True)
        return carry

    def far_step(owner, carry):
        prepare(n_tile + owner, slots + owner * cap, False)
        return carry

    load(0).wait()
    lax.fori_loop(0, n_tile, near_step, 0)
    load(1).wait()
    lax.fori_loop(0, n_tile, far_step, 0)

    live = live_ref[0]
    column_s[...] = jnp.zeros((128, 128), F32)

    def gang(step, carry, whole=True):
        made, columns = {}, []

        def place(u):
            k = step * GANG + u
            at = jnp.minimum(jnp.maximum(k, 0) if u < 0 else k, pairs_ref.shape[2] - 1)
            return pairs_ref[0, 0, at], pairs_ref[0, 1, at], ((k >= live) | (k < 0)) if u < 0 else (k >= live)

        def multiply(u):
            p, q, _ = place(u)
            made[u] = products(tall_s[p], wide_s[q], slim_s[q])

        def evaluate(u):
            p, q, dead = place(u)
            gain, heat_p, heat_q = finish(made.pop(u), seeds_s[p], factor_s[q])
            columns.append(jnp.sum(heat_p, 1, keepdims=True))
            acc[jnp.where(dead, 2 * slots, q), 16:24] += jnp.sum(heat_q.reshape(16, 8, 128), 0)
            gains[u % GANG][0:128], gains[u % GANG][128:256] = halves(gain)

        def reduce(u):
            here = [place(v) for v in (u, u + 1)]
            first, second = gains[u % GANG], gains[(u + 1) % GANG]
            weigh_p = [weigh_s[p] for p, _, _ in here]
            weigh_q = [weigh_s[q] for _, q, _ in here]
            down = jnp.concatenate([first[...], second[...]], 1)
            across = jnp.concatenate(
                [jnp.concatenate([ref[0:128], ref[128:256]], 1) for ref in (first, second)], 0
            )
            left = jnp.concatenate([jnp.concatenate([w, w], 1) for w in weigh_p], 0)
            right = jnp.concatenate([jnp.concatenate([w, w], 1) for w in weigh_q], 0)
            on_q = jnp.dot(left, down, preferred_element_type=F32)
            on_p = lax.dot_general(right, across, (((1,), (1,)), ((), ())), preferred_element_type=F32)
            for v, (p, q, dead) in enumerate(here):
                rows, lanes = slice(16 * v, 16 * v + 16), slice(128 * v, 128 * v + 128)
                acc[jnp.where(dead, 2 * slots, p), 0:16] += on_p[rows, lanes]
                acc[jnp.where(dead, 2 * slots, q), 0:16] += on_q[rows, lanes]

        def settle():
            rows = column_s[...].T
            for u in range(GANG):
                p, _, dead = place(u - GANG)
                acc[jnp.where(dead, 2 * slots, p), 16:17] += rows[u : u + 1]

        if not whole:
            for u in range(0, LAG, 2):
                reduce(u - LAG)
            settle()
            return carry

        for u in range(-AHEAD, GANG):
            if 0 <= u + AHEAD < GANG:
                multiply(u + AHEAD)
            if u >= 0:
                evaluate(u)
                if u % 2 == LAG_AT:
                    reduce(u - LAG_AT - LAG)
                if u == SETTLE_AT:
                    settle()
        column_s[:, 0:GANG] = jnp.concatenate(columns, 1)
        return carry

    gangs = lax.div(live + GANG - 1, GANG)
    lax.fori_loop(0, gangs, gang, 0)
    gang(gangs, 0, False)

    def near_out(owner, carry):
        boxed = held_ref.at[owner]
        for c in range(cap):
            sums = acc[owner * cap + c]
            heat = jnp.sum(sums[16:24], 0, keepdims=True)
            base = boxed[8 * c : 8 * c + 8] - MIDDLE
            out_ref[owner, 4 * c : 4 * c + 4] = result_rows(base, sums, heat)
        return carry

    def far_out(owner, carry):
        boxed = held_ref.at[n_tile + owner]
        for c in range(cap):
            sums = acc[slots + owner * cap + c]
            heat = jnp.sum(sums[16:24], 0, keepdims=True)
            base = boxed[8 * c : 8 * c + 8] - MIDDLE
            out_ref[n_tile + owner, 4 * c : 4 * c + 4] = result_rows(base, sums, heat)
        return carry

    lax.fori_loop(0, n_tile, near_out, 0)
    lax.fori_loop(0, n_tile, far_out, 0)


def pair_terms(n_tile, cap, pairs, live, held):
    slots = n_tile * cap
    smem = pl.BlockSpec(memory_space=pltpu.SMEM)
    vmem = pl.BlockSpec(memory_space=pltpu.VMEM)
    hbm = pl.BlockSpec(memory_space=pltpu.HBM)
    return pl.pallas_call(
        functools.partial(pair_kernel, n_tile, cap),
        out_shape=jax.ShapeDtypeStruct((2 * n_tile, 4 * cap, 128), F32),
        in_specs=[smem, smem, hbm],
        out_specs=vmem,
        scratch_shapes=[
            pltpu.VMEM(held.shape, F32),
            pltpu.SemaphoreType.DMA((2,)),
            pltpu.VMEM((slots, 128, K_WIDE), BF16),
            pltpu.VMEM((2 * slots, K_WIDE, 256), BF16),
            pltpu.VMEM((2 * slots, K_SLIM, 256), BF16),
            pltpu.VMEM((2 * slots, 16, 128), BF16),
            pltpu.VMEM((slots, 128, 128), I32),
            pltpu.VMEM((2 * slots, 1, 128), I32),
            pltpu.VMEM((2 * slots + 1, 24, 128), F32),
            pltpu.VMEM((128, 128), F32),
            *[pltpu.VMEM((256, 128), BF16)] * GANG,
        ],
        compiler_params=pltpu.CompilerParams(vmem_limit_bytes=63 * MIB),
        name="pair_terms",
    )(pairs, live, held)


def return_kernel(
    n_grp, n_tile, terms_ref, got_ref, send_sems, recv_sems, home_sem,
):
    g, t = lax.axis_index("grp"), lax.axis_index("tile")
    above, below = lax.rem(g + 1, n_grp), lax.rem(g + n_grp - 1, n_grp)
    barrier = pltpu.get_barrier_semaphore()
    for step in range(n_tile):
        owner = lax.rem(t + step, n_tile)
        if step:
            pl.semaphore_signal(barrier, inc=1, device_id=(g, owner), device_id_type=MESH)
        pl.semaphore_signal(barrier, inc=1, device_id=(above, owner), device_id_type=MESH)
    pl.semaphore_wait(barrier, 2 * n_tile - 1)

    def near(owner, slot):
        return pltpu.make_async_remote_copy(
            src_ref=terms_ref.at[owner], dst_ref=got_ref.at[slot], send_sem=send_sems.at[owner], recv_sem=recv_sems.at[slot],
            device_id=(g, owner), device_id_type=MESH,
        )

    def far(owner, slot):
        return pltpu.make_async_remote_copy(
            src_ref=terms_ref.at[n_tile + owner], dst_ref=got_ref.at[n_tile + slot], send_sem=send_sems.at[n_tile + owner],
            recv_sem=recv_sems.at[n_tile + slot], device_id=(below, owner), device_id_type=MESH,
        )

    def start(step, carry):
        owner = lax.rem(t + step, n_tile)
        far(owner, t).start()
        near(owner, t).start()
        return carry

    far(t, t).start()
    lax.fori_loop(1, n_tile, start, 0)
    home = pltpu.make_async_copy(terms_ref.at[t], got_ref.at[t], home_sem)
    home.start()
    home.wait()
    far(t, t).wait()

    def finish(step, carry):
        other = lax.rem(t + step, n_tile)
        far(other, other).wait_send()
        near(other, other).wait_send()
        far(other, other).wait_recv()
        near(other, other).wait_recv()
        return carry

    lax.fori_loop(1, n_tile, finish, 0)


def return_terms(n_grp, n_tile, terms):
    vmem = pl.BlockSpec(memory_space=pltpu.VMEM)
    hbm = pl.BlockSpec(memory_space=pltpu.HBM)
    sems = pltpu.SemaphoreType.DMA((2 * n_tile,))
    return pl.pallas_call(
        functools.partial(return_kernel, n_grp, n_tile),
        out_shape=jax.ShapeDtypeStruct(terms.shape, F32),
        in_specs=[hbm],
        out_specs=vmem,
        scratch_shapes=[sems, sems, pltpu.SemaphoreType.DMA],
        compiler_params=pltpu.CompilerParams(collective_id=1, has_side_effects=True, vmem_limit_bytes=63 * MIB),
        name="return_terms",
    )(terms)


def total_kernel(n_tile, cap, blocks, places_ref, got_ref, self_ref, out_ref, acc):
    acc[...] = self_ref[...]

    def add(worker, carry):
        for c in range(cap):
            place = places_ref[c, 0, worker]
            rows = slice(4 * c, 4 * c + 4)
            acc[place] += got_ref[worker, rows] + got_ref[n_tile + worker, rows]
        return carry

    lax.fori_loop(0, n_tile, add, 0)

    def put(b, carry):
        out_ref[:, pl.ds(pl.multiple_of(b * 128, 128), 128)] = acc[b]
        return carry

    lax.fori_loop(0, blocks, put, 0, unroll=8)


def total_terms(n_tile, cap, blocks, places, got, selfs):
    smem = pl.BlockSpec(memory_space=pltpu.SMEM)
    vmem = pl.BlockSpec(memory_space=pltpu.VMEM)
    hbm = pl.BlockSpec(memory_space=pltpu.HBM)
    return pl.pallas_call(
        functools.partial(total_kernel, n_tile, cap, blocks),
        out_shape=jax.ShapeDtypeStruct((4, blocks * 128), F32),
        in_specs=[smem, vmem, vmem],
        out_specs=vmem,
        scratch_shapes=[pltpu.VMEM((blocks, 4, 128), F32)],
        compiler_params=pltpu.CompilerParams(vmem_limit_bytes=63 * MIB),
        name="total_terms",
    )(places, got, selfs)


def per_device(
    molecule_coords,
    molecule_speeds,
    molecule_thermal_state,
    conservative_strength,
    noise_keys,
    exported_tile_places,
    tile_couplings,
    processor_coupling_tally,
):
    n_grp, n_tile = lax.axis_size("grp"), lax.axis_size("tile")
    blocks = molecule_coords.shape[1] // 128
    cap = exported_tile_places.shape[2]
    places = exported_tile_places.transpose(2, 0, 1)
    beads = (
        molecule_coords,
        molecule_speeds,
        molecule_thermal_state.reshape(blocks, 128),
        conservative_strength.reshape(blocks, 128),
        noise_keys.reshape(blocks, 128),
    )
    pairs = tile_couplings.transpose(0, 2, 1)
    held, selfs = gather_blocks(n_grp, n_tile, cap, blocks, places, *beads)
    terms = pair_terms(n_tile, cap, pairs, processor_coupling_tally, held)
    got = return_terms(n_grp, n_tile, terms)
    return total_terms(n_tile, cap, blocks, places, got, selfs)


def solution(mesh):
    in_specs = (
        P(None, ("grp", "tile")),
        P(None, ("grp", "tile")),
        P(("grp", "tile")),
        P(("grp", "tile")),
        P(("grp", "tile")),
        P(("grp", "tile"), None, None),
        P(("grp", "tile"), None, None),
        P(("grp", "tile")),
    )
    out_specs = P(None, ("grp", "tile"))
    return jax.shard_map(per_device, mesh=mesh, in_specs=in_specs, out_specs=out_specs, check_vma=False)
```
